32 devices in a mesh: seq: 8 (over z, x), batch: 4 (over y, core).
Axes of the slice: x: 2, y: 2, z: 4, core: 2. Of those that a mesh axis runs over, the one named last changes fastest.
Arguments:
- tokens: bfloat16 [4, 1024, 2048], P('batch', 'seq'), may hold values from -6 to 6
- modality: int32 [4, 1024], P('batch', 'seq'), may hold values from 0 to 2, as said below
- cotangent: bfloat16 [4, 1024, 2048], P('batch', 'seq'), may hold values from -6 to 6
- in_weight: float32 [2048, 3, 8192], P(('seq', 'batch')), may hold values from -0.125 to 0.125
- x_weight: float32 [4096, 3, 160], P(('seq', 'batch')), may hold values from -0.09375 to 0.09375
- dt_weight: float32 [4096, 3, 128], P(('seq', 'batch')), may hold values from -0.5 to 0.5
- out_weight: float32 [4096, 3, 2048], P(('seq', 'batch')), may hold values from -0.046875 to 0.046875
- norm_gain: float32 [2048, 3], P(('seq', 'batch')), may hold values from 0.5 to 1.5
- channel_params: float32 [4096, 25], P(('seq', 'batch'))
- in_first: float32 [2048, 3, 8192], P(('seq', 'batch')), may hold values from -112 to 112
- in_second: float32 [2048, 3, 8192], P(('seq', 'batch')), may hold values from 113 to 455
- x_first: float32 [4096, 3, 160], P(('seq', 'batch')), may hold values from -640 to 640
- x_second: float32 [4096, 3, 160], P(('seq', 'batch')), may hold values from 4095 to 16380
- dt_first: float32 [4096, 3, 128], P(('seq', 'batch')), may hold values from -64 to 64
- dt_second: float32 [4096, 3, 128], P(('seq', 'batch')), may hold values from 41 to 170
- out_first: float32 [4096, 3, 2048], P(('seq', 'batch')), may hold values from -320 to 320
- out_second: float32 [4096, 3, 2048], P(('seq', 'batch')), may hold values from 1023 to 4095
- gain_first: float32 [2048, 3], P(('seq', 'batch')), may hold values from -224 to 224
- gain_second: float32 [2048, 3], P(('seq', 'batch')), may hold values from 455 to 1820
- chan_first: float32 [4096, 25], P(('seq', 'batch')), may hold values from -640 to 640
- chan_second: float32 [4096, 25], P(('seq', 'batch')), may hold values from 4095 to 16380
Outputs:
- block_out: bfloat16 [4, 1024, 2048], P('batch', 'seq')
- input_grad: bfloat16 [4, 1024, 2048], P('batch', 'seq')
- in_weight_new: float32 [2048, 3, 8192], P(('seq', 'batch'))
- in_first_new: float32 [2048, 3, 8192], P(('seq', 'batch'))
- in_second_new: float32 [2048, 3, 8192], P(('seq', 'batch'))
- in_weight_low: bfloat16 [2048, 3, 8192], P(('seq', 'batch'))
- x_weight_new: float32 [4096, 3, 160], P(('seq', 'batch'))
- x_first_new: float32 [4096, 3, 160], P(('seq', 'batch'))
- x_second_new: float32 [4096, 3, 160], P(('seq', 'batch'))
- x_weight_low: bfloat16 [4096, 3, 160], P(('seq', 'batch'))
- dt_weight_new: float32 [4096, 3, 128], P(('seq', 'batch'))
- dt_first_new: float32 [4096, 3, 128], P(('seq', 'batch'))
- dt_second_new: float32 [4096, 3, 128], P(('seq', 'batch'))
- dt_weight_low: bfloat16 [4096, 3, 128], P(('seq', 'batch'))
- out_weight_new: float32 [4096, 3, 2048], P(('seq', 'batch'))
- out_first_new: float32 [4096, 3, 2048], P(('seq', 'batch'))
- out_second_new: float32 [4096, 3, 2048], P(('seq', 'batch'))
- out_weight_low: bfloat16 [4096, 3, 2048], P(('seq', 'batch'))
- gain_new: float32 [2048, 3], P(('seq', 'batch'))
- gain_first_new: float32 [2048, 3], P(('seq', 'batch'))
- gain_second_new: float32 [2048, 3], P(('seq', 'batch'))
- chan_new: float32 [4096, 25], P(('seq', 'batch'))
- chan_first_new: float32 [4096, 25], P(('seq', 'batch'))
- chan_second_new: float32 [4096, 25], P(('seq', 'batch'))
The draws below stay inside these ranges and needn't reach their ends.
Inputs may be any that keep to these rules, and one draw needn't show every extreme that they name: modality is constant over each aligned run of 128 positions of a sequence.
All inputs are finite; a program needn't handle non-finite values.
Results may differ from the reference program's by a relative error of at most 0.014.
The reference program's roundings to bfloat16 on the way count: a program that leaves them out, or rounds other values in their place, can miss the bound.
Values may be sent and summed in bfloat16 or wider, within the bound.
A program may use at most 832 MiB of HBM per device.

```python
import math
import jax
import jax.numpy as jnp
from jax import lax

D = 2048
INNER = 4096
STATE = 16
CONV = 4
RANK = 128
MODES = 3
MBLK = 128
STEP = 5
SEQLEN = 1024
BATCH = 4
CHANNELS = 25
MODE_TOK = 1365


def draw_modality(key, part):
    key = jax.random.fold_in(key, 11)
    runs = jax.random.randint(key, (BATCH, SEQLEN // MBLK), 0, MODES, dtype=jnp.int32)
    return jnp.repeat(runs, MBLK, axis=1)


def draw_channel_params(key, part):
    key = jax.random.fold_in(key, 23)
    keys = jax.random.split(key, 5)
    slowest = math.log(1.0 / (3.0 * SEQLEN))
    step_size = jnp.exp(jax.random.uniform(keys[0], (INNER, MODES), minval=math.log(0.01), maxval=math.log(0.1)))
    skip = jax.random.uniform(keys[2], (INNER, 1), minval=0.5, maxval=1.5)
    log_rates = jax.random.uniform(keys[4], (INNER, STATE), minval=slowest, maxval=0.0)
    step_bias = jnp.log(jnp.expm1(step_size))
    conv_bias = 0.3 * jax.random.normal(keys[1], (INNER, 1))
    conv_taps = 0.5 * jax.random.normal(keys[3], (INNER, CONV))
    return jnp.concatenate([step_bias, conv_bias, skip, conv_taps, log_rates], 1).astype(jnp.float32)


def block_scale(rng, extent, shards, smallest, high):
    def one(position, blocks):
        heights = jax.random.uniform(jax.random.fold_in(jax.random.fold_in(rng, 6), position), (blocks,), jnp.float32, smallest / len(shards), high / len(shards))
        return jnp.repeat(jnp.exp(heights), extent[position] // blocks).reshape((-1,) + (1,) * (len(extent) - position - 1))

    loudness = one(*shards[0])
    for cut in shards[1:]:
        loudness = loudness * one(*cut)
    return loudness


def bell_draw(key, shape, spread, most, cuts=(), kind=jnp.bfloat16):
    level = block_scale(key, shape, cuts, -0.22, 0.18) if cuts else 1.0
    drawn = jax.random.normal(key, shape, jnp.float32) * spread * level
    return jnp.minimum(jnp.maximum(drawn, -most), most).astype(kind)


def setup_inputs(seed: int = 0) -> dict:
    splits = jax.random.split(jax.random.key(seed), 22)
    return {
        "tokens": bell_draw(splits[0], (BATCH, SEQLEN, D), 1.0, 6.0, ((0, 4), (1, 8))),
        "modality": draw_modality(jax.random.fold_in(splits[21], 71), 0),
        "cotangent": bell_draw(splits[2], (BATCH, SEQLEN, D), 1.0, 6.0, ((0, 4), (1, 8))),
        "in_weight": bell_draw(splits[3], (D, MODES, 2 * INNER), D ** -0.5, 0.125, ((0, 32),), jnp.float32),
        "x_weight": bell_draw(splits[4], (INNER, MODES, RANK + 2 * STATE), INNER ** -0.5, 0.09375, ((0, 32),), jnp.float32),
        "dt_weight": bell_draw(splits[5], (INNER, MODES, RANK), RANK ** -0.5, 0.5, ((0, 32),), jnp.float32),
        "out_weight": bell_draw(splits[6], (INNER, MODES, D), (4 * INNER) ** -0.5, 0.046875, ((0, 32),), jnp.float32),
        "norm_gain": jnp.clip(1.0 + 0.1 * jax.random.normal(splits[7], (D, MODES), jnp.float32), 0.5, 1.5),
        "channel_params": draw_channel_params(jax.random.fold_in(splits[21], 71), 0),
        "in_first": bell_draw(splits[9], (D, MODES, 2 * INNER), (0.5 * MODE_TOK ** 0.5), 112.0, ((0, 32),), jnp.float32),
        "in_second": jnp.clip(jnp.exp(math.log(455.0) - 1.3929096 * jax.random.uniform(splits[10], (D, MODES, 2 * INNER), jnp.float32) ** block_scale(splits[10], (D, MODES, 2 * INNER), ((0, 32),), -0.2, 0.2)), 113.0, 455.0),
        "x_first": bell_draw(splits[11], (INNER, MODES, RANK + 2 * STATE), (3 * MODE_TOK ** 0.5), 640.0, ((0, 32),), jnp.float32),
        "x_second": jnp.clip(jnp.exp(math.log(16380.0) - 1.3862944 * jax.random.uniform(splits[12], (INNER, MODES, RANK + 2 * STATE), jnp.float32) ** block_scale(splits[12], (INNER, MODES, RANK + 2 * STATE), ((0, 32),), -0.2, 0.2)), 4095.0, 16380.0),
        "dt_first": bell_draw(splits[13], (INNER, MODES, RANK), (0.3 * MODE_TOK ** 0.5), 64.0, ((0, 32),), jnp.float32),
        "dt_second": jnp.clip(jnp.exp(math.log(170.0) - 1.4222264 * jax.random.uniform(splits[14], (INNER, MODES, RANK), jnp.float32) ** block_scale(splits[14], (INNER, MODES, RANK), ((0, 32),), -0.2, 0.2)), 41.0, 170.0),
        "out_first": bell_draw(splits[15], (INNER, MODES, D), (1.5 * MODE_TOK ** 0.5), 320.0, ((0, 32),), jnp.float32),
        "out_second": jnp.clip(jnp.exp(math.log(4095.0) - 1.38702723 * jax.random.uniform(splits[16], (INNER, MODES, D), jnp.float32) ** block_scale(splits[16], (INNER, MODES, D), ((0, 32),), -0.2, 0.2)), 1023.0, 4095.0),
        "gain_first": bell_draw(splits[17], (D, MODES), (MODE_TOK ** 0.5), 224.0, ((0, 32),), jnp.float32),
        "gain_second": jnp.clip(jnp.exp(math.log(1820.0) - 1.3862944 * jax.random.uniform(splits[18], (D, MODES), jnp.float32) ** block_scale(splits[18], (D, MODES), ((0, 32),), -0.2, 0.2)), 455.0, 1820.0),
        "chan_first": bell_draw(splits[19], (INNER, CHANNELS), (3 * MODE_TOK ** 0.5), 640.0, ((0, 32),), jnp.float32),
        "chan_second": jnp.clip(jnp.exp(math.log(16380.0) - 1.3862944 * jax.random.uniform(splits[20], (INNER, CHANNELS), jnp.float32) ** block_scale(splits[20], (INNER, CHANNELS), ((0, 32),), -0.2, 0.2)), 4095.0, 16380.0),
    }


NORM_EPS = 1e-05
BETA_ONE = 0.5
BETA_TWO = 0.75
ADAM_EPS = 1e-08
DECAY = 0.01
SMALL_RATE = 0.1
CHAN_RATE = 2.0
HIGHEST = lax.Precision.HIGHEST

@jax.custom_vjp
def low(v):
    return lax.optimization_barrier(v.astype(jnp.bfloat16)).astype(jnp.float32)

@jax.custom_vjp
def low_back(v):
    return v

def low_keep(v):
    return (low(v), None)

def low_pass(kept, grad):
    return (grad,)

def back_keep(v):
    return (v, None)

def back_low(kept, grad):
    return (low(grad),)
low.defvjp(low_keep, low_pass)
low_back.defvjp(back_keep, back_low)

def moded(left, weights, one_hot, flip):
    width = weights.shape[0] if flip else weights.shape[2]
    total = jnp.zeros(left.shape[:2] + (width,), left.dtype)
    for mode in range(MODES):
        matrix = weights[:, mode, :]
        if flip:
            part = jnp.einsum('blk,fk->blf', left, matrix, precision=HIGHEST)
        else:
            part = jnp.einsum('blk,kf->blf', left, matrix, precision=HIGHEST)
        total = total + one_hot[:, :, mode:mode + 1] * part
    return total

def selective_scan(steps, drives, entry, leave, rates):
    batch = steps.shape[0]
    length = steps.shape[1]
    span = 64

    def one_step(state, inputs):
        step_now, drive_now, entry_now, leave_now = inputs
        state = jnp.exp(step_now[:, :, None] * rates[None]) * state + drive_now[:, :, None] * entry_now[:, None, :]
        return (state, lax.optimization_barrier(jnp.sum(state * leave_now[:, None, :], -1)))

    def block_scan(state, inputs):
        return lax.scan(one_step, state, inputs)
    pieces = tuple((jnp.swapaxes(part, 0, 1).reshape(length // span, span, batch, part.shape[2]) for part in (steps, drives, entry, leave)))
    start = jnp.zeros((batch, steps.shape[2], entry.shape[2]), steps.dtype)
    _, outs = lax.scan(jax.checkpoint(block_scan), start, pieces)
    return jnp.swapaxes(outs.reshape(length, batch, -1), 0, 1)

def adam_update(weight, first, second, grad, rate):
    first_new = BETA_ONE * first + (1.0 - BETA_ONE) * grad
    second_new = BETA_TWO * second + (1.0 - BETA_TWO) * grad * grad
    first_hat = first_new / (1.0 - BETA_ONE ** STEP)
    second_hat = second_new / (1.0 - BETA_TWO ** STEP)
    weight_new = weight - rate * (first_hat / (jnp.sqrt(second_hat) + ADAM_EPS) + DECAY * weight)
    return (weight_new, first_new, second_new)

def reference(tokens, modality, cotangent, in_weight, x_weight, dt_weight, out_weight, norm_gain, channel_params, in_first, in_second, x_first, x_second, dt_first, dt_second, out_first, out_second, gain_first, gain_second, chan_first, chan_second):
    one_hot = (modality[:, :, None] == jnp.arange(MODES, dtype=jnp.int32)[None, None, :]).astype(jnp.float32)

    def forward(x_in, in_matrix, x_matrix, dt_matrix, out_matrix, gain, chan):
        in_matrix = low(in_matrix)
        x_matrix = low(x_matrix)
        dt_matrix = low(dt_matrix)
        out_matrix = low(out_matrix)
        gain = low(gain)
        chan = low(chan)
        step_bias = chan[:, :MODES]
        conv_bias = chan[:, MODES]
        skip = chan[:, MODES + 1]
        conv_taps = chan[:, MODES + 2:MODES + 2 + CONV]
        log_rates = chan[:, MODES + 2 + CONV:]
        rates = -jnp.exp(log_rates)
        scale = lax.rsqrt(lax.optimization_barrier(jnp.mean(x_in * x_in, -1, keepdims=True)) + NORM_EPS)
        token_gain = jnp.einsum('blm,dm->bld', one_hot, gain, precision=HIGHEST)
        normal = low(x_in * scale * token_gain)
        joint = low_back(moded(normal, in_matrix, one_hot, False))
        inner = low(joint[:, :, :INNER])
        gate = joint[:, :, INNER:]
        length = x_in.shape[1]
        padded = jnp.pad(inner, ((0, 0), (CONV - 1, 0), (0, 0)))
        pre = conv_bias
        for k in range(CONV):
            pre = pre + conv_taps[:, k] * padded[:, k:k + length]
        act = low(jax.nn.silu(pre))
        projected = low_back(moded(act, x_matrix, one_hot, False))
        rank_part = low(projected[:, :, :RANK])
        entry = projected[:, :, RANK:RANK + STATE]
        leave = projected[:, :, RANK + STATE:]
        step_raw = low_back(moded(rank_part, dt_matrix, one_hot, True))
        steps = jax.nn.softplus(step_raw + jnp.einsum('blm,em->ble', one_hot, step_bias, precision=HIGHEST))
        scanned = selective_scan(steps, steps * act, entry, leave, rates)
        mixed = low((scanned + skip * act) * jax.nn.silu(gate))
        return x_in + moded(mixed, out_matrix, one_hot, False)
    x_rows = tokens.astype(jnp.float32)
    result, backward = jax.vjp(forward, x_rows, in_weight, x_weight, dt_weight, out_weight, norm_gain, channel_params)
    grads = backward(cotangent.astype(jnp.float32))
    in_new = adam_update(in_weight, in_first, in_second, grads[1], D ** (-0.5))
    x_new = adam_update(x_weight, x_first, x_second, grads[2], INNER ** (-0.5))
    dt_new = adam_update(dt_weight, dt_first, dt_second, grads[3], RANK ** (-0.5))
    out_new = adam_update(out_weight, out_first, out_second, grads[4], (4 * INNER) ** (-0.5))
    gain_new = adam_update(norm_gain, gain_first, gain_second, grads[5], SMALL_RATE)
    chan_new = adam_update(channel_params, chan_first, chan_second, grads[6], CHAN_RATE)
    return (result.astype(jnp.bfloat16), grads[0].astype(jnp.bfloat16), in_new[0], in_new[1], in_new[2], in_new[0].astype(jnp.bfloat16), x_new[0], x_new[1], x_new[2], x_new[0].astype(jnp.bfloat16), dt_new[0], dt_new[1], dt_new[2], dt_new[0].astype(jnp.bfloat16), out_new[0], out_new[1], out_new[2], out_new[0].astype(jnp.bfloat16), gain_new[0], gain_new[1], gain_new[2], chan_new[0], chan_new[1], chan_new[2])
```

```python
import functools

import jax
import jax.numpy as jnp
import numpy as np
from jax import lax
from jax.experimental import pallas as pl
from jax.experimental.pallas import tpu as pltpu
from jax.sharding import Mesh
from jax.sharding import PartitionSpec as P

D = 2048
INNER = 4096
STATE = 16
CONV = 4
RANK = 128
MODES = 3
MBLK = 128
STEP = 5
XCOLS = RANK + 2 * STATE
GROUPS = 16

NORM_EPS = 1e-05
BETA_ONE = 0.5
BETA_TWO = 0.75
ADAM_EPS = 1e-08
DECAY = 0.01
SMALL_RATE = 0.1
CHAN_RATE = 2.0
LN2 = 0.6931471805599453
F32 = jnp.float32
BF16 = jnp.bfloat16

EVERY = ("seq", "hi", "lo")
GROUP = ("seq", "hi")
VMEM = pltpu.VMEM
MIB = 1024 * 1024


def adam_update(weight, first, second, grad, rate):
    first_new = BETA_ONE * first + (1.0 - BETA_ONE) * grad
    second_new = BETA_TWO * second + (1.0 - BETA_TWO) * grad * grad
    first_hat = first_new / (1.0 - BETA_ONE**STEP)
    second_hat = second_new / (1.0 - BETA_TWO**STEP)
    weight_new = weight - rate * (first_hat / (jnp.sqrt(second_hat) + ADAM_EPS) + DECAY * weight)
    return (weight_new, first_new, second_new)


def nt_dot(left, right):
    return lax.dot_general(left, right, (((1,), (1,)), ((), ())), preferred_element_type=F32)


def tn_dot(left, right):
    return lax.dot_general(left, right, (((0,), (0,)), ((), ())), preferred_element_type=F32)


def nn_dot(left, right):
    return jnp.dot(left, right, preferred_element_type=F32)


def add_outer(total_ref, mode, x_ref, q, right):
    piece = 512
    for k in range(D // piece):
        at = slice(k * piece, (k + 1) * piece)
        total_ref[mode, at, :] += tn_dot(x_ref[q, :, at], right)


def sigmoid(v):
    return 1.0 / (1.0 + jnp.exp(-v))


def rounded(v):
    return lax.reduce_precision(v, 8, 7)


def softplus(v):
    return jnp.maximum(v, 0.0) + jnp.log1p(jnp.exp(-jnp.abs(v)))


class Plan:
    def __init__(self, blocks, seqs, channels):
        self.nb = blocks
        self.seqs = seqs
        self.chan = channels
        self.halves = channels // 128
        self.fold = 8 // self.seqs
        self.groups = STATE // self.fold
        self.held = self.groups * self.halves

    def sub(self, f, q):
        return f * self.seqs + q

    def select(self):
        out = np.zeros((self.fold, 2 * STATE, 128), np.float32)
        for f in range(self.fold):
            for g in range(self.groups):
                out[f, g * self.fold + f, g] = 1.0
                out[f, STATE + g * self.fold + f, self.groups + g] = 1.0
        return out

    def summers(self):
        entry = np.zeros((self.groups * 128, 128), np.float32)
        leave = np.zeros((self.groups * 128, 128), np.float32)
        for g in range(self.groups):
            entry[g * 128 : (g + 1) * 128, g] = 1.0
            leave[g * 128 : (g + 1) * 128, self.groups + g] = 1.0
        return entry, leave

    def fold_rates(self, rates):
        shaped = rates.reshape(self.groups, self.fold, 1, self.halves, 128).transpose(3, 0, 1, 2, 4)
        wide = jnp.broadcast_to(shaped, (self.halves, self.groups, self.fold, self.seqs, 128))
        return wide.reshape(self.held, 8, 128)


NX = 2

PAR_SBIAS = 0
PAR_CBIAS = MODES
PAR_SKIP = MODES + 1
PAR_TAPS = MODES + 2
PAR_RATES = MODES + 2 + CONV
PAR_ROWS = 32
SUM_LOG = 8


def params_of(shape_like):
    return pltpu.CompilerParams(vmem_limit_bytes=shape_like * MIB)


def whole(shape):
    return pl.BlockSpec(shape, lambda *_: (0,) * len(shape), pipeline_mode=pl.Buffered(1))


def kept(shape):
    return pl.BlockSpec(shape, lambda *_: (0,) * len(shape))


def packed(index, seqs):
    return pl.BlockSpec((seqs, XCOLS, MBLK), index)


def packed_shape(blocks, kind=BF16):
    return jax.ShapeDtypeStruct((blocks, XCOLS, MBLK), kind)


def front_kernel(
    plan, modes, x_ref, w_ref, wx_ref, par_ref, inner_ref, gate_ref, pre_ref, act_ref, proj_ref, halo
):
    j = pl.program_id(0)
    channels = plan.chan

    @pl.when(j == 0)
    def _():
        halo[...] = jnp.zeros_like(halo)

    for q in range(plan.seqs):
        mode = modes[j * plan.seqs + q]
        joint = nn_dot(x_ref[q], w_ref[mode])
        inner_low = joint[:, :channels].astype(BF16)
        gate_ref[q] = joint[:, channels:]
        inner_ref[q] = inner_low
        inner = inner_low.astype(F32)
        wide = jnp.concatenate([halo[q], inner], 0)
        halo[q] = inner[MBLK - 8 :]
        pre = par_ref[PAR_CBIAS : PAR_CBIAS + 1, :]
        for k in range(CONV):
            pre = pre + par_ref[PAR_TAPS + k : PAR_TAPS + k + 1, :] * wide[5 + k : 5 + k + MBLK]
        pre_ref[q] = pre
        act_low = (pre * sigmoid(pre)).astype(BF16)
        act_ref[q] = act_low
        proj_ref[q, :MBLK] = nt_dot(act_low, wx_ref[mode, :RANK]).astype(BF16)
        proj_ref[q, MBLK:] = nt_dot(wx_ref[mode, RANK:], act_low).astype(BF16)


def front(plan, modes, normal, w_in, w_x, par):
    nb, seqs, chan = plan.nb, plan.seqs, plan.chan

    def rows(width):
        return pl.BlockSpec((seqs, MBLK, width), lambda j, *_: (j, 0, 0))

    def out(width, kind):
        return jax.ShapeDtypeStruct((nb * seqs, MBLK, width), kind)

    return pl.pallas_call(
        functools.partial(front_kernel, plan),
        grid_spec=pltpu.PrefetchScalarGridSpec(
            num_scalar_prefetch=1,
            grid=(nb,),
            in_specs=[rows(D), whole(w_in.shape), whole(w_x.shape), whole(par.shape)],
            out_specs=[rows(chan), rows(chan), rows(chan), rows(chan), packed(lambda j, *_: (j, 0, 0), seqs)],
            scratch_shapes=[VMEM((seqs, 8, chan), F32)],
        ),
        out_shape=[out(chan, BF16), out(chan, F32), out(chan, F32), out(chan, BF16), packed_shape(nb * seqs)],
        compiler_params=params_of(60),
        cost_estimate=pl.CostEstimate(
            flops=2 * nb * seqs * MBLK * D * 2 * chan, bytes_accessed=24 * MIB, transcendentals=0
        ),
        name="front",
    )(modes, normal, w_in, w_x, par)


def step_inputs(plan, mode, proj, wdt_ref, par_ref):
    rank_low = proj[:MBLK]
    raw = nt_dot(rank_low, wdt_ref[mode])
    biased = raw + par_ref[pl.ds(PAR_SBIAS + mode, 1), :]
    return rank_low, biased


def scan_kernel(
    plan, modes, proj_ref, act_ref, gate_ref, wdt_ref, wout_ref, par_ref, rates_ref, sel_ref,
    scanned_ref, mixed_ref, before_ref, last_ref, *refs,
):
    part_refs, (st, dr, el, yy, state) = refs[:-5], refs[-5:]
    j = pl.program_id(0)
    groups = plan.groups
    count = plan.nb * plan.seqs
    here_x, here_y = modes[count], modes[count + 1]

    @pl.when(j == 0)
    def _():
        state[...] = jnp.zeros_like(state)

    for q in range(plan.seqs):
        mode = modes[j * plan.seqs + q]
        proj = proj_ref[q]
        _, biased = step_inputs(plan, mode, proj, wdt_ref, par_ref)
        steps = softplus(biased)
        drive = steps * act_ref[q].astype(F32)
        for f in range(plan.fold):
            at = pl.ds(plan.sub(f, q), MBLK, stride=8)
            el[at, :] = tn_dot(proj[MBLK:], sel_ref[f])
            for c in range(plan.halves):
                st[c, at, :] = steps[:, c * 128 : (c + 1) * 128]
                dr[c, at, :] = drive[:, c * 128 : (c + 1) * 128]

    unroll = 16

    def some_steps(i, carry):
        now = list(carry)
        for u in range(unroll):
            t = i * unroll + u
            rows = pl.ds(pl.multiple_of(t * 8, 8), 8)
            pair = el[rows, :]
            entry = [jnp.broadcast_to(pair[:, g : g + 1], (8, 128)) for g in range(groups)]
            leave = [jnp.broadcast_to(pair[:, groups + g : groups + g + 1], (8, 128)) for g in range(groups)]
            for c in range(plan.halves):
                step = st[c, rows, :]
                drive = dr[c, rows, :]
                total = None
                for g in range(groups):
                    v = c * groups + g
                    before_ref[t, v] = now[v]
                    now[v] = jnp.exp2(step * rates_ref[v]) * now[v] + drive * entry[g]
                    term = now[v] * leave[g]
                    total = term if total is None else total + term
                yy[c, rows, :] = total
        return tuple(now)

    final = lax.fori_loop(0, MBLK // unroll, some_steps, tuple(state[v] for v in range(plan.held)))
    for v in range(plan.held):
        state[v] = final[v]
        last_ref[v] = final[v]

    skip = par_ref[PAR_SKIP : PAR_SKIP + 1, :]
    for q in range(plan.seqs):
        mode = modes[j * plan.seqs + q]
        parts = []
        for c in range(plan.halves):
            total = yy[c, pl.ds(plan.sub(0, q), MBLK, stride=8), :]
            for f in range(1, plan.fold):
                total = total + yy[c, pl.ds(plan.sub(f, q), MBLK, stride=8), :]
            parts.append(total)
        scanned = parts[0] if len(parts) == 1 else jnp.concatenate(parts, 1)
        scanned_ref[q] = scanned
        gate = gate_ref[q]
        mixed = ((scanned + skip * act_ref[q].astype(F32)) * (gate * sigmoid(gate))).astype(BF16)
        mixed_ref[q] = mixed
        dx = lax.rem(lax.rem(j, NX) + here_x, NX)
        dy = lax.rem(q + here_y, plan.seqs)
        product = nn_dot(mixed, wout_ref[mode]).astype(BF16)
        for r, part_ref in enumerate(part_refs):

            @pl.when(dx * plan.seqs + dy == r)
            def _():
                part_ref[0] = product


def forward_scan(plan, modes, proj, act, gate, w_dt, w_out, par, rates, select):
    nb, seqs, chan, held = plan.nb, plan.seqs, plan.chan, plan.held
    halves = VMEM((plan.halves, MBLK * 8, 128), F32)
    plane = NX * seqs

    def rows(width):
        return pl.BlockSpec((seqs, MBLK, width), lambda j, *_: (j, 0, 0))

    def out(width, kind):
        return jax.ShapeDtypeStruct((nb * seqs, MBLK, width), kind)

    return pl.pallas_call(
        functools.partial(scan_kernel, plan),
        grid_spec=pltpu.PrefetchScalarGridSpec(
            num_scalar_prefetch=1,
            grid=(nb,),
            in_specs=[
                packed(lambda j, *_: (j, 0, 0), seqs), rows(chan), rows(chan), whole(w_dt.shape), whole(w_out.shape),
                whole(par.shape), whole(rates.shape), whole(select.shape),
            ],
            out_specs=[
                rows(chan), rows(chan),
                pl.BlockSpec((MBLK, held, 8, 128), lambda j, *_: (j, 0, 0, 0)),
                kept((held, 8, 128)),
                *[pl.BlockSpec((1, MBLK, D), lambda j, *_: (j // NX, 0, 0))] * plane,
            ],
            scratch_shapes=[halves, halves, VMEM((MBLK * 8, 128), F32), halves, VMEM((held, 8, 128), F32)],
        ),
        out_shape=[
            out(chan, F32), out(chan, BF16),
            jax.ShapeDtypeStruct((nb * MBLK, held, 8, 128), F32),
            jax.ShapeDtypeStruct((held, 8, 128), F32),
            *[jax.ShapeDtypeStruct((nb // NX, MBLK, D), BF16)] * plane,
        ],
        compiler_params=params_of(60),
        cost_estimate=pl.CostEstimate(
            flops=60 * nb * MBLK * held * 1024, bytes_accessed=150 * MIB, transcendentals=nb * MBLK * held * 1024
        ),
        name="forward_scan",
    )(modes, proj, act, gate, w_dt, w_out, par, rates, select)


def back_kernel(
    plan, modes, cot_ref, x_ref, proj_ref, act_ref, gate_ref, scanned_ref, mixed_ref, before_ref, last_ref,
    wdt_ref, wout_ref, par_ref, rates_ref, sel_ref, sume_ref, suml_ref,
    bact_ref, bgate_ref, bproj_ref, dtg_ref, outg_ref, ing_ref, sums_ref,
    logr_ref, st, dr, el, bs, aa, uu, pe, plv, carry_ref, after_ref,
):
    i = pl.program_id(0)
    j = plan.nb - 1 - i
    groups = plan.groups

    @pl.when(i == 0)
    def _():
        carry_ref[...] = jnp.zeros_like(carry_ref)
        after_ref[...] = last_ref[...]
        dtg_ref[...] = jnp.zeros_like(dtg_ref)
        outg_ref[...] = jnp.zeros_like(outg_ref)
        ing_ref[...] = jnp.zeros_like(ing_ref)
        sums_ref[...] = jnp.zeros_like(sums_ref)
        logr_ref[...] = jnp.zeros_like(logr_ref)

    skip = par_ref[PAR_SKIP : PAR_SKIP + 1, :]
    held = []
    for q in range(plan.seqs):
        mode = modes[j * plan.seqs + q]
        proj = proj_ref[q]
        rank_low, biased = step_inputs(plan, mode, proj, wdt_ref, par_ref)
        steps = softplus(biased)
        act = act_ref[q].astype(F32)
        drive = steps * act
        back_mixed = nt_dot(cot_ref[q], wout_ref[mode])
        gate = gate_ref[q]
        sig = sigmoid(gate)
        back_scanned = back_mixed * (gate * sig)
        slope = sig * (1.0 + gate * (1.0 - sig))
        back_gate = (back_mixed * (scanned_ref[q] + skip * act) * slope).astype(BF16)
        bgate_ref[q] = back_gate
        add_outer(ing_ref, mode, x_ref, q, back_gate)
        outg_ref[mode] += tn_dot(mixed_ref[q], cot_ref[q])
        for f in range(plan.fold):
            at = pl.ds(plan.sub(f, q), MBLK, stride=8)
            el[at, :] = tn_dot(proj[MBLK:], sel_ref[f])
            for c in range(plan.halves):
                cols = slice(c * 128, (c + 1) * 128)
                st[c, at, :] = steps[:, cols]
                dr[c, at, :] = drive[:, cols]
                bs[c, at, :] = back_scanned[:, cols]
        held.append((mode, rank_low, biased, steps, act, back_scanned))

    unroll = 16

    def some_steps(i, carry):
        lam_in = list(carry[0])
        after = list(carry[1])
        log_sum = list(carry[2])
        for u in range(unroll):
            t = MBLK - 1 - (i * unroll + u)
            rows = pl.ds(pl.multiple_of(t * 8, 8), 8)
            pair = el[rows, :]
            entry = [jnp.broadcast_to(pair[:, g : g + 1], (8, 128)) for g in range(groups)]
            leave = [jnp.broadcast_to(pair[:, groups + g : groups + g + 1], (8, 128)) for g in range(groups)]
            entry_sum, leave_sum = [None] * groups, [None] * groups
            for c in range(plan.halves):
                step = st[c, rows, :]
                drive = dr[c, rows, :]
                push = bs[c, rows, :]
                a_sum = None
                u_sum = None
                for g in range(groups):
                    v = c * groups + g
                    rate = rates_ref[v]
                    before = before_ref[t, v]
                    lam = push * leave[g] + lam_in[v]
                    leave_term = push * after[v]
                    entry_term = lam * drive
                    leave_sum[g] = leave_term if c == 0 else leave_sum[g] + leave_term
                    entry_sum[g] = entry_term if c == 0 else entry_sum[g] + entry_term
                    moved = lam * jnp.exp2(step * rate)
                    lam_in[v] = moved
                    after[v] = before
                    felt = moved * before
                    a_term = rate * felt
                    u_term = lam * entry[g]
                    a_sum = a_term if a_sum is None else a_sum + a_term
                    u_sum = u_term if u_sum is None else u_sum + u_term
                    log_sum[v] = log_sum[v] + step * felt
                aa[c, rows, :] = a_sum
                uu[c, rows, :] = u_sum
            for g in range(groups):
                cols = slice(g * 128, (g + 1) * 128)
                pe[rows, cols] = entry_sum[g]
                plv[rows, cols] = leave_sum[g]
        return (tuple(lam_in), tuple(after), tuple(log_sum))

    start = (
        tuple(carry_ref[v] for v in range(plan.held)),
        tuple(after_ref[v] for v in range(plan.held)),
        tuple(logr_ref[v] for v in range(plan.held)),
    )
    lam_end, after_end, log_end = lax.fori_loop(0, MBLK // unroll, some_steps, start)
    for v in range(plan.held):
        carry_ref[v] = lam_end[v]
        after_ref[v] = after_end[v]
        logr_ref[v] = log_end[v]

    el[...] = nn_dot(pe[...].astype(BF16), sume_ref[...]) + nn_dot(plv[...].astype(BF16), suml_ref[...])

    for q in range(plan.seqs):
        mode, rank_low, biased, steps, act, back_scanned = held[q]
        a_parts, u_parts = [], []
        back_pair = jnp.zeros((2 * STATE, MBLK), F32)
        for c in range(plan.halves):
            a_total, u_total = None, None
            for f in range(plan.fold):
                at = pl.ds(plan.sub(f, q), MBLK, stride=8)
                a_term, u_term = aa[c, at, :], uu[c, at, :]
                a_total = a_term if a_total is None else a_total + a_term
                u_total = u_term if u_total is None else u_total + u_term
            a_parts.append(a_total * LN2)
            u_parts.append(u_total)
        for f in range(plan.fold):
            both = el[pl.ds(plan.sub(f, q), MBLK, stride=8), :]
            back_pair = back_pair + nt_dot(sel_ref[f], both.astype(BF16))
        a_all = a_parts[0] if len(a_parts) == 1 else jnp.concatenate(a_parts, 1)
        u_all = u_parts[0] if len(u_parts) == 1 else jnp.concatenate(u_parts, 1)
        back_steps = a_all + act * u_all
        bact_ref[q] = skip * back_scanned + steps * u_all
        back_pre_step = back_steps * sigmoid(biased)
        raw_low = back_pre_step.astype(BF16)
        bproj_ref[q, :MBLK] = nn_dot(raw_low, wdt_ref[mode]).astype(BF16)
        bproj_ref[q, MBLK:] = back_pair.astype(BF16)
        dtg_ref[mode] += tn_dot(raw_low, rank_low)
        sums_ref[pl.ds(mode, 1), :] += jnp.sum(back_pre_step, 0, keepdims=True)
        sums_ref[MODES : MODES + 1, :] += jnp.sum(back_scanned * act, 0, keepdims=True)

    @pl.when(j == 0)
    def _():
        for v in range(plan.held):
            c, g = v // groups, v % groups
            for f in range(plan.fold):
                at = plan.sub(f, 0)
                total = jnp.sum(logr_ref[v, at : at + plan.seqs, :], 0, keepdims=True)
                n = SUM_LOG + g * plan.fold + f
                scaled = total * rates_ref[v, at : at + 1, :] * LN2
                sums_ref[n : n + 1, c * 128 : (c + 1) * 128] = scaled


def backward_scan(plan, modes, cot, normal, proj, act, gate, scanned, mixed, before, last, w_dt, w_out, par, rates, select):
    nb, seqs, chan, groups, held = plan.nb, plan.seqs, plan.chan, plan.groups, plan.held
    sum_entry, sum_leave = plan.summers()
    sum_entry, sum_leave = jnp.asarray(sum_entry, BF16), jnp.asarray(sum_leave, BF16)

    def rows(width):
        return pl.BlockSpec((seqs, MBLK, width), lambda i, *_: (nb - 1 - i, 0, 0))

    def out(width, kind):
        return jax.ShapeDtypeStruct((nb * seqs, MBLK, width), kind)

    tall = VMEM((plan.halves, MBLK * 8, 128), F32)
    return pl.pallas_call(
        functools.partial(back_kernel, plan),
        grid_spec=pltpu.PrefetchScalarGridSpec(
            num_scalar_prefetch=1,
            grid=(nb,),
            in_specs=[
                rows(D), rows(D), packed(lambda i, *_: (nb - 1 - i, 0, 0), seqs),
                rows(chan), rows(chan), rows(chan), rows(chan),
                pl.BlockSpec((MBLK, held, 8, 128), lambda i, *_: (nb - 1 - i, 0, 0, 0)),
                whole(last.shape), whole(w_dt.shape), whole(w_out.shape), whole(par.shape),
                whole(rates.shape), whole(select.shape),
                whole(sum_entry.shape), whole(sum_leave.shape),
            ],
            out_specs=[
                rows(chan), rows(chan), packed(lambda i, *_: (nb - 1 - i, 0, 0), seqs),
                kept((MODES, chan, RANK)), kept((MODES, chan, D)), kept((MODES, D, chan)),
                kept((SUM_LOG + STATE, chan)),
            ],
            scratch_shapes=[
                VMEM((held, 8, 128), F32), tall, tall, VMEM((MBLK * 8, 128), F32), tall, tall, tall,
                VMEM((MBLK * 8, groups * 128), F32), VMEM((MBLK * 8, groups * 128), F32),
                VMEM((held, 8, 128), F32), VMEM((held, 8, 128), F32),
            ],
        ),
        out_shape=[
            out(chan, F32), out(chan, BF16), packed_shape(nb * seqs),
            jax.ShapeDtypeStruct((MODES, chan, RANK), F32),
            jax.ShapeDtypeStruct((MODES, chan, D), F32),
            jax.ShapeDtypeStruct((MODES, D, chan), F32),
            jax.ShapeDtypeStruct((SUM_LOG + STATE, chan), F32),
        ],
        compiler_params=params_of(60),
        cost_estimate=pl.CostEstimate(
            flops=100 * nb * MBLK * held * 1024, bytes_accessed=300 * MIB, transcendentals=nb * MBLK * held * 1024
        ),
        name="backward_scan",
    )(modes, cot, normal, proj, act, gate, scanned, mixed, before, last, w_dt, w_out, par, rates, select,
      sum_entry, sum_leave)


def tail_kernel(
    plan, modes, bp_ref, bact_ref, bgate_ref, pre_ref, act_ref, inner_ref, earlier_ref, x_ref,
    wx_ref, par_ref,
    joint_ref, ing_ref, xg_ref, sums_ref,
    halo,
):
    i = pl.program_id(0)
    j = plan.nb - 1 - i
    channels = plan.chan

    @pl.when(i == 0)
    def _():
        halo[...] = jnp.zeros_like(halo)
        ing_ref[...] = jnp.zeros_like(ing_ref)
        xg_ref[...] = jnp.zeros_like(xg_ref)
        sums_ref[...] = jnp.zeros_like(sums_ref)

    first = jnp.where(j == 0, 0.0, 1.0)
    for q in range(plan.seqs):
        mode = modes[j * plan.seqs + q]
        rank_low, pair_low = bp_ref[q, :MBLK], bp_ref[q, MBLK:]
        back_act = bact_ref[q] + nn_dot(rank_low, wx_ref[mode, :RANK]) + tn_dot(pair_low, wx_ref[mode, RANK:])
        xg_ref[mode, :RANK] += tn_dot(rank_low, act_ref[q])
        xg_ref[mode, RANK:] += nn_dot(pair_low, act_ref[q])
        pre = pre_ref[q]
        sig = sigmoid(pre)
        back_pre = back_act * (sig * (1.0 + pre * (1.0 - sig)))
        wide = jnp.concatenate([back_pre, halo[q]], 0)
        halo[q] = back_pre[:8]
        inner_wide = jnp.concatenate(
            [earlier_ref[q][MBLK - 16 :].astype(F32) * first, inner_ref[q].astype(F32)], 0
        )
        back_inner = None
        for k in range(CONV):
            term = par_ref[PAR_TAPS + k : PAR_TAPS + k + 1, :] * wide[CONV - 1 - k : CONV - 1 - k + MBLK]
            back_inner = term if back_inner is None else back_inner + term
            felt = back_pre * inner_wide[13 + k : 13 + k + MBLK]
            sums_ref[k : k + 1, :] += jnp.sum(felt, 0, keepdims=True)
        sums_ref[CONV : CONV + 1, :] += jnp.sum(back_pre, 0, keepdims=True)
        inner_low = back_inner.astype(BF16)
        joint_low = jnp.concatenate([inner_low, bgate_ref[q]], 1)
        joint_ref[q] = joint_low
        add_outer(ing_ref, mode, x_ref, q, inner_low)


def tail(plan, modes, bp, bact, bgate, pre, act, inner, normal, w_x, par):
    nb, seqs, chan = plan.nb, plan.seqs, plan.chan

    def rows(width):
        return pl.BlockSpec((seqs, MBLK, width), lambda i, *_: (nb - 1 - i, 0, 0))

    return pl.pallas_call(
        functools.partial(tail_kernel, plan),
        grid_spec=pltpu.PrefetchScalarGridSpec(
            num_scalar_prefetch=1,
            grid=(nb,),
            in_specs=[
                packed(lambda i, *_: (nb - 1 - i, 0, 0), seqs), rows(chan), rows(chan), rows(chan), rows(chan), rows(chan),
                pl.BlockSpec((seqs, MBLK, chan), lambda i, *_: (jnp.maximum(nb - 2 - i, 0), 0, 0)),
                rows(D), whole(w_x.shape), whole(par.shape),
            ],
            out_specs=[
                rows(2 * chan), kept((MODES, D, chan)), kept((MODES, XCOLS, chan)),
                kept((8, chan)),
            ],
            scratch_shapes=[VMEM((seqs, 8, chan), F32)],
        ),
        out_shape=[
            jax.ShapeDtypeStruct((nb * seqs, MBLK, 2 * chan), BF16),
            jax.ShapeDtypeStruct((MODES, D, chan), F32),
            jax.ShapeDtypeStruct((MODES, XCOLS, chan), F32),
            jax.ShapeDtypeStruct((8, chan), F32),
        ],
        compiler_params=params_of(60),
        cost_estimate=pl.CostEstimate(
            flops=4 * nb * seqs * MBLK * D * 2 * chan, bytes_accessed=40 * MIB, transcendentals=0
        ),
        name="tail",
    )(modes, bp, bact, bgate, pre, act, inner, inner, normal, w_x, par)


ANY = pl.ANY
DMA = pltpu.SemaphoreType.DMA


def any_spec():
    return pl.BlockSpec(memory_space=ANY)


def vmem_spec():
    return pl.BlockSpec(memory_space=VMEM)


def remote(src, dst, send, recv, device):
    return pltpu.make_async_remote_copy(
        src_ref=src, dst_ref=dst, send_sem=send, recv_sem=recv, device_id=device,
        device_id_type=pl.DeviceIdType.MESH,
    )


class Place:
    def __init__(self, dims):
        self.ns, self.ny, self.nl = dims
        self.nz = self.ns // NX
        self.groups = self.ns * self.ny
        self.devices = self.groups * self.nl
        seq = lax.axis_index("seq")
        self.z, self.x = lax.div(seq, NX), lax.rem(seq, NX)
        self.y = lax.axis_index("hi")
        self.l = lax.axis_index("lo")
        self.g = seq * self.ny + self.y
        self.i = self.g * self.nl + self.l
        self.ox, self.oy = NX - 1 - self.x, self.ny - 1 - self.y

    def device(self, z, x, y, low):
        return (z * NX + x, y, low)

    def of_group(self, g, low):
        return (lax.div(g, self.ny), lax.rem(g, self.ny), low)

    def of_index(self, i):
        return self.of_group(lax.div(i, self.nl), lax.rem(i, self.nl))

    def group(self, z, x, y):
        return (z * NX + x) * self.ny + y

    def relative(self, n, sign):
        plane = NX * self.ny
        dz, rest = lax.div(n, plane), lax.rem(n, plane)
        dx, dy = lax.div(rest, self.ny), lax.rem(rest, self.ny)
        z = lax.rem(self.z + self.nz + sign * dz, self.nz)
        x = lax.rem(self.x + NX + sign * dx, NX)
        y = lax.rem(self.y + self.ny + sign * dy, self.ny)
        return self.group(z, x, y)

    def in_plane(self, z, r):
        x = lax.rem(self.x + lax.div(r, self.ny), NX)
        y = lax.rem(self.y + lax.rem(r, self.ny), self.ny)
        return self.group(z, x, y)

    def after(self, n):
        return self.relative(jnp.int32(n), 1)

    def before(self, n):
        return self.relative(jnp.int32(n), -1)

    def x_peer(self):
        return self.device(self.z, self.ox, self.y, self.l)

    def y_peer(self):
        return self.device(self.z, self.x, self.oy, self.l)

    def z_after(self, k):
        return lax.rem(self.z + k, self.nz)

    def z_before(self, k):
        return lax.rem(self.z + self.nz - k, self.nz)

    def z_peer(self, k):
        return self.device(self.z_after(k), self.x, self.y, self.l)

    def low_after(self, k):
        return lax.rem(self.l + k, self.nl)

    def low_before(self, k):
        return lax.rem(self.l + self.nl - k, self.nl)

    def low_peer(self, k):
        return self.device(self.z, self.x, self.y, self.low_after(k))


def lanes_shape(rows, parts, width):
    return (rows, parts * width) if width % 128 == 0 else (parts, rows, width)


def lanes_at(ref, part, width):
    if width % 128 == 0:
        return ref.at[:, pl.ds(pl.multiple_of(part * width, width), width)]
    return ref.at[part]


def lanes_join(array):
    return array if array.ndim == 2 else jnp.swapaxes(array, 0, 1).reshape(array.shape[1], -1)


def lanes_split(array, parts):
    width = array.shape[1] // parts
    return array if width % 128 == 0 else array.reshape(array.shape[0], parts, width).swapaxes(0, 1)


def greet_all(here):
    barrier = pltpu.get_barrier_semaphore()

    def greet(k, carry):
        peer = here.of_index(lax.rem(here.i + k, here.devices))
        pl.semaphore_signal(barrier, inc=1, device_id=peer, device_id_type=pl.DeviceIdType.MESH)
        return carry

    lax.fori_loop(1, here.devices, greet, 0)
    pl.semaphore_wait(barrier, here.devices - 1)


def greet_near(here, low_too):
    barrier = pltpu.get_barrier_semaphore()
    peers = [here.x_peer()]
    if here.ny > 1:
        peers.append(here.y_peer())
    peers += [here.z_peer(k) for k in range(1, here.nz)]
    if low_too:
        peers += [here.low_peer(k) for k in range(1, here.nl)]
    for peer in peers:
        pl.semaphore_signal(barrier, inc=1, device_id=peer, device_id_type=pl.DeviceIdType.MESH)
    pl.semaphore_wait(barrier, len(peers))


def gather_sems(dims):
    nz = dims[0] // NX
    return [DMA((1,))] + [DMA((nz, 2))] * 6


def in_line(dims):
    return dims[0] // NX <= 4


class Gather:
    def __init__(self, here, own, out, rows, sems, line):
        self.here, self.own, self.out, self.half, self.line = here, own, out, rows // 2, line
        self.local, self.up, self.down, self.xs, self.ys, self.fx, self.fy = sems

    def block(self, z, x, y):
        return self.out.at[self.here.group(z, x, y)]

    def mine(self, z):
        return self.block(z, self.here.x, self.here.y)

    def keep(self):
        return pltpu.make_async_copy(self.own, self.out.at[self.here.g], self.local.at[0])

    def next(self, src, dst, sems, d, step):
        here = self.here
        peer = here.device(here.z + step, here.x, here.y, here.l)
        return remote(src, dst, sems.at[d, 0], sems.at[d, 1], peer)

    def far(self, k):
        here = self.here
        return remote(self.own, self.out.at[here.g], self.up.at[k, 0], self.up.at[k, 1], here.z_peer(k))

    def cross(self, z, src):
        here = self.here
        dst = self.mine(z)
        out = [remote(src, dst, self.xs.at[z, 0], self.xs.at[z, 1], here.x_peer())]
        if here.ny > 1:
            out.append(remote(src, dst, self.ys.at[z, 0], self.ys.at[z, 1], here.y_peer()))
        return out

    def spread(self, z, src):
        for copy in self.cross(z, src):
            copy.start()

    def start(self):
        here = self.here
        self.keep().start()
        if self.line:
            at = self.out.at[here.g]

            @pl.when(here.z + 1 < here.nz)
            def _():
                self.next(self.own, at, self.up, 0, 1).start()

            @pl.when(here.z > 0)
            def _():
                self.next(self.own, at, self.down, 0, -1).start()

        else:
            for k in range(1, here.nz):
                self.far(k).start()
        self.spread(here.z, self.own)

    def step(self, d):
        here = self.here
        if not self.line:
            z = here.z_before(d)
            self.far(d).wait_recv()
            self.spread(z, self.mine(z))
            return
        for sems, sign in ((self.up, 1), (self.down, -1)):
            z = here.z - sign * d
            on = here.z + sign

            @pl.when((z >= 0) & (z < here.nz))
            def _():
                got = self.mine(z)
                self.next(got, got, sems, d - 1, -sign).wait_recv()

                @pl.when((on >= 0) & (on < here.nz))
                def _():
                    self.next(got, got, sems, d, sign).start()

                self.spread(z, got)

    def halves(self, z, first):
        here = self.here
        to_y = self.block(z, here.ox, here.y) if first else self.block(z, here.ox, here.oy)
        to_x = self.block(z, here.x, here.oy) if first else self.block(z, here.ox, here.oy)
        upper, lower = to_y.at[pl.ds(0, self.half)], to_x.at[pl.ds(self.half, self.half)]
        return (
            remote(upper, upper, self.fy.at[z, 0], self.fy.at[z, 1], here.y_peer()),
            remote(lower, lower, self.fx.at[z, 0], self.fx.at[z, 1], here.x_peer()),
        )

    def forward(self, z):
        here = self.here
        copies = self.cross(z, self.mine(z))
        copies[0].wait_recv()
        if here.ny > 1:
            to_y, to_x = self.halves(z, True)
            to_y.start()
            copies[1].wait_recv()
            to_x.start()

    def forward_all(self):
        here = self.here
        self.forward(here.z)
        for d in range(1, here.nz):
            if self.line:
                for z in (here.z - d, here.z + d):

                    @pl.when((z >= 0) & (z < here.nz))
                    def _():
                        self.forward(z)

            else:
                self.forward(here.z_before(d))

    def end(self):
        here = self.here
        self.keep().wait()

        def finish(z, carry):
            for copy in self.cross(z, self.mine(z)):
                copy.wait_send()
            if here.ny > 1:
                for copy in self.halves(z, False):
                    copy.wait()
            return carry

        lax.fori_loop(0, here.nz, finish, 0)
        if not self.line:
            for k in range(1, here.nz):
                self.far(k).wait_send()
            return
        for sems, sign in ((self.up, 1), (self.down, -1)):
            on = here.z + sign
            for d in range(here.nz):
                z = here.z - sign * d

                @pl.when((z >= 0) & (z < here.nz) & (on >= 0) & (on < here.nz))
                def _():
                    self.next(self.mine(z), self.mine(z), sems, d, sign).wait_send()


def reduce_scratch(dims, rows, width, kind):
    ns, ny, _ = dims
    nz = ns // NX
    ra = rows // 2 if ny > 1 else rows
    rb = rows // 2
    out = [
        VMEM((nz, ny, ra, width), kind), VMEM((rows, width), F32),
        VMEM((nz, rows, width), kind), VMEM((nz, rows, width), kind),
        VMEM((1, 16, 128), kind),
        DMA((nz, 2)), DMA((nz, 2)), DMA((nz, 2)), DMA((nz, 2)), DMA((nz, 2)), DMA((nz, 2)),
    ]
    if ny > 1:
        out += [VMEM((nz, NX, rb, width), kind)] + [VMEM((nz, rb, width), kind)] * 4
    return out


class Reduce:
    def __init__(self, here, part, rows, bufs, line):
        self.here, self.part, self.line = here, part, line
        self.r1a, self.acc, self.s3, self.r3, self.r3d = bufs[:5]
        self.s1, self.s1b, self.s2, self.s2b, self.up, self.down = bufs[5:11]
        self.two = here.ny > 1
        ra = rows // 2 if self.two else rows
        self.top, self.low = pl.ds(0, ra), pl.ds(ra, rows - ra)
        if self.two:
            self.r1b, self.t2a, self.r2a, self.t2b, self.r2b = bufs[11:]

    def target(self, k):
        if not self.line:
            return self.here.z_after(k + 1)
        k = jnp.int32(k)
        half = lax.div(k, 2)
        return jnp.where(lax.rem(k, 2) == 0, self.here.nz - 1 - half, half)

    def copies(self, k):
        here, part, z = self.here, self.part, self.target(k)
        out = [remote(part.at[z, here.ox, :, self.top], self.r1a.at[k], self.s1.at[k, 0], self.s1.at[k, 1], here.x_peer())]
        if self.two:
            out.append(
                remote(part.at[z, :, here.oy, self.low], self.r1b.at[k], self.s1b.at[k, 0], self.s1b.at[k, 1], here.y_peer())
            )
        return out

    def crossed(self, k):
        here = self.here
        return (
            remote(self.t2a.at[k], self.r2a.at[k], self.s2.at[k, 0], self.s2.at[k, 1], here.y_peer()),
            remote(self.t2b.at[k], self.r2b.at[k], self.s2b.at[k, 0], self.s2b.at[k, 1], here.x_peer()),
        )

    def first(self, k):
        for copy in self.copies(k):
            copy.start()

    def second(self, k):
        here, part, z = self.here, self.part, self.target(k)
        kind = part.dtype
        copies = self.copies(k)
        copies[0].wait_recv()
        if self.two:
            total = part[z, here.x, here.oy, self.top].astype(F32) + self.r1a[k, here.oy].astype(F32)
            self.t2a[k] = total.astype(kind)
            a, b = self.crossed(k)
            a.start()
            copies[1].wait_recv()
            total = part[z, here.ox, here.y, self.low].astype(F32) + self.r1b[k, here.ox].astype(F32)
            self.t2b[k] = total.astype(kind)
            b.start()

    def totals(self, k):
        here, part, z = self.here, self.part, self.target(k)
        out = [(self.top, part[z, here.x, here.y, self.top].astype(F32) + self.r1a[k, here.y].astype(F32))]
        if self.two:
            for copy in self.crossed(k):
                copy.wait_recv()
            lower = part[z, here.x, here.y, self.low].astype(F32) + self.r1b[k, here.x].astype(F32)
            out = [(self.top, out[0][1] + self.r2a[k].astype(F32)), (self.low, lower + self.r2b[k].astype(F32))]
        return out

    def flows(self):
        return ((self.up, self.r3, 1), (self.down, self.r3d, -1))

    def along(self, z, sems, slot, step):
        here = self.here
        peer = here.device(here.z + step, here.x, here.y, here.l)
        return remote(self.s3.at[z], slot.at[z], sems.at[z, 0], sems.at[z, 1], peer)

    def straight(self, k):
        return remote(self.s3.at[k], self.r3.at[k], self.up.at[k, 0], self.up.at[k, 1], self.here.z_peer(k + 1))

    def third(self, k):
        here = self.here
        kind = self.part.dtype
        z = self.target(k)
        if not self.line:
            for rows, total in self.totals(k):
                self.s3[k, rows] = total.astype(kind)
            self.straight(k).start()
            return

        @pl.when(z == here.z)
        def _():
            for rows, total in self.totals(k):
                self.acc[rows] = total

        for sems, slot, sign in self.flows():
            back = here.z - sign

            @pl.when(sign * (z - here.z) > 0)
            def _():
                totals = self.totals(k)

                @pl.when((back >= 0) & (back < here.nz))
                def _():
                    self.along(z, sems, slot, -sign).wait_recv()
                    for rows, total in totals:
                        self.s3[z, rows] = (total + slot[z, rows].astype(F32)).astype(kind)

                @pl.when((back < 0) | (back >= here.nz))
                def _():
                    for rows, total in totals:
                        self.s3[z, rows] = total.astype(kind)

                self.along(z, sems, slot, sign).start()

    def last(self):
        here = self.here
        if not self.line:
            for rows, total in self.totals(here.nz - 1):
                self.acc[rows] = total

            def add(k, carry):
                self.straight(k).wait_recv()
                self.acc[...] += self.r3[k].astype(F32)
                return carry

            lax.fori_loop(0, here.nz - 1, add, 0)
            return
        for sems, slot, sign in self.flows():
            back = here.z - sign

            @pl.when((back >= 0) & (back < here.nz))
            def _():
                self.along(here.z, sems, slot, -sign).wait_recv()
                self.acc[...] += slot[here.z].astype(F32)

    def end(self):
        here = self.here

        def finish(k, carry):
            for copy in self.copies(k):
                copy.wait_send()
            if self.two:
                for copy in self.crossed(k):
                    copy.wait_send()
            return carry

        lax.fori_loop(0, here.nz, finish, 0)
        if not self.line:
            for k in range(here.nz - 1):
                self.straight(k).wait_send()
            return
        for z in range(here.nz):
            for sems, slot, sign in self.flows():

                @pl.when(sign * (z - here.z) > 0)
                def _():
                    self.along(z, sems, slot, sign).wait_send()


def comm_params(name_id, mib):
    return pltpu.CompilerParams(collective_id=name_id, has_side_effects=True, vmem_limit_bytes=mib * MIB)


def comm_cost(us):
    return pl.CostEstimate(flops=0, bytes_accessed=us * 3_000_000, transcendentals=0)


def entry_kernel(
    dims, small_ref, pick_ref, x_ref, win_ref, wdt_ref, wout_ref, wx_ref, chan_ref,
    modes_out, gain_out, normal_out, win_out, wdt_out, wout_out, wx_out, chan_out,
    slots, own, smalls, cols, keep, lows, weights, *gathers,
):
    here = Place(dims)
    rows_d = win_ref.shape[1]
    rows_e = wdt_ref.shape[1]
    chan = win_out.shape[2] // 2
    greet_all(here)

    def small_copy(k):
        peer = here.of_index(lax.rem(here.i + k, here.devices))
        return remote(small_ref, slots.at[here.i], smalls.at[k, 0], smalls.at[k, 1], peer)

    def send_small(k, carry):
        small_copy(k).start()
        return carry

    lax.fori_loop(1, here.devices, send_small, 0)
    slots[here.i] = small_ref[...]

    def rows_of(g, low):
        return win_out.at[:, pl.ds(pl.multiple_of((g * here.nl + low) * rows_d, rows_d), rows_d), :]

    def cols_of(g):
        dst = rows_of(here.g, here.l)
        out = []
        for side in range(2):
            at = pl.ds(pl.multiple_of(side * INNER + g * chan, chan), chan)
            out.append((win_ref.at[:, :, at], dst.at[:, :, pl.ds(side * chan, chan)]))
        return out

    def send_cols(z, r):
        g = here.in_plane(z, r)
        for side, (src, dst) in enumerate(cols_of(g)):
            to = cols.at[side, z * plane + r, 0]
            there = cols.at[side, here.z * plane + r, 1]
            remote(src, dst, to, there, here.of_group(g, here.l)).start()

    plane = NX * here.ny

    def own_copies():
        out = [
            pltpu.make_async_copy(src, dst, keep.at[5 * side]) for side, (src, dst) in enumerate(cols_of(here.g))
        ]
        for n, (src, dst) in enumerate(shared(here.l)):
            out.append(pltpu.make_async_copy(src, dst, keep.at[n + 1]))
        return out

    def shared(low):
        rows = pl.ds(pl.multiple_of(low * rows_e, rows_e), rows_e)
        return (
            (wdt_ref, wdt_out.at[:, rows, :]),
            (wout_ref, wout_out.at[:, rows, :]),
            (wx_ref, lanes_at(wx_out, low, rows_e)),
            (chan_ref, lanes_at(chan_out, low, rows_e)),
        )

    def low_copies(k):
        peer = here.low_peer(k)
        return [
            remote(src, dst, weights.at[k, n, 0], weights.at[k, n, 1], peer)
            for n, (src, dst) in enumerate(shared(here.l))
        ]

    def own_forward(k):
        return [
            remote(src, dst, lows.at[k, here.g + side * here.groups, 0], lows.at[k, here.g + side * here.groups, 1], here.low_peer(k))
            for side, (src, dst) in enumerate(cols_of(here.g))
        ]

    def col_forward(k, n, src_group, src):
        return remote(src, rows_of(src_group, here.l), lows.at[k, n, 0], lows.at[k, n, 1], here.low_peer(k))

    for copy in own_copies():
        copy.start()
    for k in range(1, here.nl):
        for copy in low_copies(k) + own_forward(k):
            copy.start()

    def wait_small(k, carry):
        small_copy(k).wait_recv()
        return carry

    lax.fori_loop(1, here.devices, wait_small, 0)
    lane = lax.broadcasted_iota(jnp.int32, (1, 128), 1)
    row = jnp.zeros((1, 128), F32)
    for g in range(here.groups):
        row = jnp.where(lane == g, slots[g * here.nl + here.l, MODES : MODES + 1, :], row)
    modes_out[...] = jnp.broadcast_to(row, (8, 128))
    x = x_ref[...].astype(F32)
    scale = lax.rsqrt(jnp.mean(x * x, -1, keepdims=True) + NORM_EPS)
    per = 128 // rows_d
    for t in range(D // 128):
        tile = slots[t * per]
        for n in range(1, per):
            tile = tile + slots[t * per + n]
        row = jnp.sum(tile * pick_ref[...], 0, keepdims=True)
        at = slice(t * 128, (t + 1) * 128)
        gain_out[:, at] = jnp.broadcast_to(row, (8, 128))
        own[:, at] = (x[:, at] * scale * row).astype(BF16)

    gather = Gather(here, own, normal_out, MBLK, gathers, in_line(dims))
    gather.start()

    def send_plane(d):
        def one(r, carry):
            z = jnp.where(lax.rem(r, 2) == 0, here.z_after(d), here.z_before(d))

            @pl.when((z != here.z) | (r > 0))
            def _():
                send_cols(z, r)

            return carry

        lax.fori_loop(0, plane, one, 0)

    send_plane(0)
    for d in range(1, here.nz):
        gather.step(d)
        send_plane(d)
    gather.forward_all()

    def each_source(act):
        def one(n, carry):
            z, r = lax.div(n, plane), lax.rem(n, plane)

            @pl.when((z != here.z) | (r > 0))
            def _():
                act(n, here.in_plane(z, r))

            return carry

        lax.fori_loop(0, here.groups, one, 0)

    def pass_cols(n, g):
        got = rows_of(g, here.l)
        for side in range(2):
            half = got.at[:, :, pl.ds(side * chan, chan)]
            remote(half, half, cols.at[side, n, 0], cols.at[side, n, 1], here.of_group(g, here.l)).wait_recv()
        for k in range(1, here.nl):
            col_forward(k, g, g, got).start()

    each_source(pass_cols)
    gather.end()

    def end_lows(n, g):
        for k in range(1, here.nl):
            mine, theirs = rows_of(g, here.l), rows_of(g, here.low_before(k))
            remote(mine, mine, lows.at[k, g, 0], lows.at[k, g, 1], here.low_peer(k)).wait_send()
            remote(theirs, theirs, lows.at[k, g, 0], lows.at[k, g, 1], here.low_peer(k)).wait_recv()

    def end_sent(n, g):
        for side in range(2):
            half = rows_of(g, here.l).at[:, :, pl.ds(side * chan, chan)]
            remote(half, half, cols.at[side, n, 0], cols.at[side, n, 1], here.x_peer()).wait_send()

    for k in range(1, here.nl):
        for copy in own_forward(k):
            copy.wait()

    def end_small(k, carry):
        small_copy(k).wait_send()
        return carry

    each_source(end_lows)
    each_source(end_sent)
    lax.fori_loop(1, here.devices, end_small, 0)
    for copy in own_copies():
        copy.wait()
    for k in range(1, here.nl):
        for n, (_, got) in enumerate(shared(here.low_before(k))):
            remote(got, got, weights.at[k, n, 0], weights.at[k, n, 1], here.low_peer(k)).wait()


def entry(dims, small, pick, x, win, wdt, wout, wx, chan):
    ns, ny, nl = dims
    groups, devices = ns * ny, ns * ny * nl
    shape = jax.ShapeDtypeStruct

    def tall(ref):
        return shape((MODES, ref.shape[1] * nl, ref.shape[2]), BF16)

    return pl.pallas_call(
        functools.partial(entry_kernel, dims),
        in_specs=[vmem_spec()] * 3 + [any_spec()] * 5,
        out_specs=[vmem_spec()] * 2 + [any_spec()] * 6,
        out_shape=[
            shape((8, 128), F32), shape((8, D), F32), shape((groups, MBLK, D), BF16),
            shape((MODES, D, win.shape[2] // groups), BF16), tall(wdt), tall(wout),
            *[shape(lanes_shape(a.shape[0], nl, a.shape[1]), a.dtype) for a in (wx, chan)],
        ],
        scratch_shapes=[
            VMEM((devices, 8, 128), F32), VMEM((MBLK, D), BF16), DMA((devices, 2)), DMA((2, groups, 2)),
            DMA((6,)), DMA((nl, 2 * groups, 2)), DMA((nl, 4, 2)), *gather_sems(dims),
        ],
        compiler_params=comm_params(1, 60),
        cost_estimate=comm_cost(100),
        name="entry",
    )(small, pick, x, win, wdt, wout, wx, chan)


def column_scratch(dims, rows_d, chan):
    ns, ny, nl = dims
    piece = (ns * ny, MODES, rows_d, chan)
    return [VMEM(piece, F32), VMEM((nl - 1,) + piece, F32), DMA((ns * ny,)), DMA((nl, ns * ny, 2))]


class Columns:
    def __init__(self, here, src, bufs):
        self.here, self.src = here, src
        self.mine, self.theirs, self.keep, self.swap = bufs

    def own_copy(self, n):
        here = self.here
        return pltpu.make_async_copy(self.src.at[:, here.after(n), here.l], self.mine.at[n], self.keep.at[n])

    def swap_copy(self, k, n):
        here = self.here
        part = self.src.at[:, here.after(n), here.low_after(k)]
        sems = self.swap.at[k, n]
        return remote(part, self.theirs.at[k - 1, n], sems.at[0], sems.at[1], here.low_peer(k))

    def begin(self):
        def one(n, carry):
            self.own_copy(n).start()
            for k in range(1, self.here.nl):
                self.swap_copy(k, n).start()
            return carry

        lax.fori_loop(0, self.here.groups, one, 0)

    def merged(self, n):
        self.own_copy(n).wait()
        total = self.mine[n]
        for k in range(1, self.here.nl):
            self.swap_copy(k, n).wait_recv()
            total = total + self.theirs[k - 1, n]
        return total.astype(BF16)

    def end(self):
        def one(n, carry):
            for k in range(1, self.here.nl):
                self.swap_copy(k, n).wait_send()
            return carry

        lax.fori_loop(0, self.here.groups, one, 0)


def share_kernel(dims, extras, part_ref, *refs):
    here = Place(dims)
    nz, plane = here.nz, NX * here.ny
    more = len(column_scratch(dims, 16, 128)) if extras else 0
    extra_in, refs = refs[:extras], refs[extras:]
    out_ref, extra_out, refs = refs[0], refs[1 : extras + 1], refs[extras + 1 :]
    near, sent, far, res, near_sems, far_sems, back_sems, wide_sems, keep, pairs = refs[:10]
    columns = refs[10 : 10 + more]
    spot = here.x * here.ny + here.y

    def partner(r):
        x = lax.rem(here.x + r // here.ny, NX)
        y = lax.rem(here.y + r % here.ny, here.ny)
        return x * here.ny + y, here.device(here.z, x, y, here.l)

    barrier = pltpu.get_barrier_semaphore()
    peers = [partner(r)[1] for r in range(1, plane)] + [here.z_peer(k) for k in range(1, nz)]
    if extras:
        peers += [here.low_peer(k) for k in range(1, here.nl)]
    for peer in peers:
        pl.semaphore_signal(barrier, inc=1, device_id=peer, device_id_type=pl.DeviceIdType.MESH)
    pl.semaphore_wait(barrier, len(peers))

    def to_near(r):
        at, peer = partner(r)
        return remote(part_ref.at[:, at], near.at[r - 1], near_sems.at[r, 0], near_sems.at[r, 1], peer)

    def to_far(k):
        return remote(sent.at[here.z_after(k)], far.at[k - 1], far_sems.at[k, 0], far_sems.at[k, 1], here.z_peer(k))

    def back_far(k, z):
        return remote(res, out_ref.at[z, spot], back_sems.at[k, 0], back_sems.at[k, 1], here.z_peer(k))

    def back_near(r, at):
        src = out_ref.at[:, spot]
        return remote(src, out_ref.at[:, at], wide_sems.at[r, 0], wide_sems.at[r, 1], partner(r)[1])

    def swaps(k):
        to = here.low_after(k)
        return [
            remote(src.at[:, to], dst.at[k - 1], pairs.at[k, n, 0], pairs.at[k, n, 1], here.low_peer(k))
            for n, (src, dst) in enumerate(zip(extra_in[1:], extra_out[1:]))
        ]

    for r in range(1, plane):
        to_near(r).start()
    for r in range(1, plane):
        to_near(r).wait_recv()

    def total(z):
        out = part_ref[z, spot].astype(F32)
        for r in range(1, plane):
            out = out + near[r - 1, z].astype(F32)
        return out

    for k in range(1, nz):
        z = here.z_after(k)
        sent[z] = total(z).astype(BF16)
        to_far(k).start()
    if extras:
        column = Columns(here, extra_in[0], columns)
        column.begin()
    mine = total(here.z)
    for k in range(1, nz):
        to_far(k).wait_recv()
        mine = mine + far[k - 1].astype(F32)
    res[...] = mine.astype(BF16)
    own = pltpu.make_async_copy(res, out_ref.at[here.z, spot], keep.at[0])
    own.start()
    for k in range(1, nz):
        back_far(k, here.z).start()
    own.wait()
    for k in range(1, nz):
        back_far(k, here.z_before(k)).wait_recv()
    for r in range(1, plane):
        back_near(r, spot).start()
    if extras:

        def merge(n, carry):
            extra_out[0][here.after(n)] = column.merged(n)
            return carry

        lax.fori_loop(0, here.groups, merge, 0)
    for r in range(1, plane):
        back_near(r, partner(r)[0]).wait()
        to_near(r).wait_send()
    for k in range(1, nz):
        to_far(k).wait_send()
        back_far(k, here.z).wait_send()
    if extras:
        column.end()
        for k in range(1, here.nl):
            for copy in swaps(k):
                copy.wait()


def share(dims, name_id, part, extras=()):
    ns, ny, nl = dims
    nz, plane = ns // NX, NX * ny
    shape = jax.ShapeDtypeStruct
    block = (XCOLS, MBLK)
    far = [shape((nl - 1, e.shape[0]) + e.shape[2:], F32) for e in extras[1:]]
    far_specs = [any_spec()] * len(far)
    if extras:
        far = [shape((ns * ny, MODES) + extras[0].shape[3:], BF16)] + far
        far_specs = [vmem_spec()] + far_specs
    return pl.pallas_call(
        functools.partial(share_kernel, dims, len(extras)),
        in_specs=[vmem_spec()] + [any_spec()] * len(extras),
        out_specs=[any_spec()] + far_specs,
        out_shape=[shape((nz, plane) + block, BF16)] + far,
        scratch_shapes=[
            VMEM((plane - 1, nz) + block, BF16), VMEM((nz,) + block, BF16), VMEM((nz - 1,) + block, BF16),
            VMEM(block, BF16), DMA((plane, 2)), DMA((nz, 2)), DMA((nz, 2)), DMA((plane, 2)), DMA((1,)),
            DMA((nl, max(len(extras), 1), 2)),
        ]
        + (column_scratch(dims, extras[0].shape[3], extras[0].shape[4]) if extras else []),
        compiler_params=comm_params(name_id, 60),
        cost_estimate=comm_cost(30),
        name="share",
    )(part.reshape((nz, plane) + block), *extras)


class Staged:
    def __init__(self, dims, parts):
        self.ns, self.ny, _ = dims
        self.nz = self.ns // NX
        self.parts = parts
        self.z = lax.axis_index("seq") // NX

    def plane(self):
        out = []
        for r in range(1, NX * self.ny):
            dx, dy = r // self.ny, r % self.ny
            moves = []
            for g in range(self.ns * self.ny):
                z, x, y = g // self.ny // NX, g // self.ny % NX, g % self.ny
                moves.append((g, (z * NX + (x + dx) % NX) * self.ny + (y + dy) % self.ny))
            out.append(lax.ppermute(self.parts[r], GROUP, moves))
        return out

    def line(self, got):
        total = self.parts[0].astype(F32)
        for piece in got:
            total = total + piece.astype(F32)
        return total.astype(BF16)

    def along(self, line):
        out = [lax.dynamic_index_in_dim(line, self.z, 0, keepdims=False)]
        for k in range(1, self.nz):
            moves = [(s, ((s // NX + k) % self.nz) * NX + s % NX) for s in range(self.ns)]
            piece = lax.dynamic_index_in_dim(line, (self.z + k) % self.nz, 0, keepdims=False)
            out.append(lax.ppermute(piece, "seq", moves))
        return out


def exit_kernel(
    dims, modes_ref, joint_ref, w_ref, ing_ref, dtg_ref, outg_ref, xg_ref, suma_ref, sumb_ref,
    x_ref, cot_ref, gain_ref, pick_ref,
    grad_out, gsum_out, ing_out, dtg_out, outg_out, xg_out, suma_out, sumb_out,
    part_ref, gparts, gslots, ready, pairs, smalls, cols, *bufs,
):
    here = Place(dims)
    rows_d, chan = ing_ref.shape[3], ing_ref.shape[4]
    rows_e = dtg_ref.shape[2]
    more = len(column_scratch(dims, 16, 128))
    columns, bufs = bufs[:more], bufs[more:]
    greet_all(here)
    nz, plane = here.nz, NX * here.ny
    reduce = Reduce(here, part_ref, MBLK, bufs, False)
    column = Columns(here, ing_ref, columns)

    def landing(g):
        return ing_out.at[:, :, pl.ds(pl.multiple_of(g * chan, chan), chan)]

    def col_copy(n, g):
        return remote(ready.at[n], landing(g), cols.at[n, 0], cols.at[n, 1], here.of_group(here.after(n), here.l))

    def own_copy():
        return pltpu.make_async_copy(ready.at[0], landing(here.g), cols.at[0, 0])

    def send_inner(n, carry):
        ready[n] = column.merged(n)
        col_copy(n, here.g).start()
        return carry

    def pair_copies(k):
        to = here.low_after(k)
        peer = here.low_peer(k)
        out = []
        for n, (src, dst) in enumerate(((dtg_ref, dtg_out), (outg_ref, outg_out))):
            out.append(remote(src.at[:, to], dst.at[k - 1], pairs.at[k, n, 0], pairs.at[k, n, 1], peer))
        for n, (src, dst) in enumerate(((xg_ref, xg_out), (suma_ref, suma_out), (sumb_ref, sumb_out))):
            sems = pairs.at[k, n + 2]
            out.append(remote(lanes_at(src, to, rows_e), dst.at[k - 1], sems.at[0], sems.at[1], peer))
        return out

    def first(k):
        z = reduce.target(k)

        def one(p, carry):
            x, y = lax.div(p, here.ny), lax.rem(p, here.ny)
            block = here.group(z, x, y)
            product = nt_dot(joint_ref[block], w_ref[modes_ref[block]])
            part_ref[z, x, y] = product.astype(BF16)
            return carry

        lax.fori_loop(0, plane, one, 0)
        reduce.first(k)

    first(0)
    first(1)
    column.begin()
    for k in range(nz):
        if k + 2 < nz:
            first(k + 2)
        if k == 1:
            for low in range(1, here.nl):
                for copy in pair_copies(low):
                    copy.start()
        reduce.second(k)
        if k > 0:
            reduce.third(k - 1)
        lax.fori_loop(max(k * plane, 1), (k + 1) * plane, send_inner, 0)
    ready[0] = column.merged(0)
    own_copy().start()
    reduce.last()

    acc = reduce.acc
    x = x_ref[...].astype(F32)
    scale = lax.rsqrt(jnp.mean(x * x, -1, keepdims=True) + NORM_EPS)
    back = acc[...]
    weighted = back * gain_ref[0:1, :]
    dots = jnp.mean(weighted * x, -1, keepdims=True)
    back_x = scale * weighted - x * (scale * scale * scale) * dots
    grad_out[...] = (cot_ref[...].astype(F32) + back_x).astype(BF16)
    felt = jnp.sum(back * x * scale, 0, keepdims=True)
    for t in range(D // 128):
        gparts[t] = felt[:, t * 128 : (t + 1) * 128] * pick_ref[...]

    def small_copy(k):
        i = lax.rem(here.i + k, here.devices)
        src = gparts.at[lax.div(i * rows_d, 128)]
        return remote(src, gslots.at[here.i], smalls.at[k, 0], smalls.at[k, 1], here.of_index(i))

    def send_small(k, carry):
        small_copy(k).start()
        return carry

    lax.fori_loop(1, here.devices, send_small, 0)
    gslots[here.i] = gparts[lax.div(here.i * rows_d, 128)]
    reduce.end()
    column.end()
    for k in range(1, here.nl):
        for copy in pair_copies(k):
            copy.wait()
    own_copy().wait()

    def end_cols(n, carry):
        col_copy(n, here.before(n)).wait()
        return carry

    lax.fori_loop(1, here.groups, end_cols, 0)

    def end_small(k, carry):
        small_copy(k).wait()
        return carry

    lax.fori_loop(1, here.devices, end_small, 0)
    gsum_out[...] = jnp.sum(gslots[...], 0)


def leave(dims, modes, joint, w_in, ing, swapped, rest, x, cot, gain, pick):
    ns, ny, nl = dims
    groups, devices = ns * ny, ns * ny * nl
    shape = jax.ShapeDtypeStruct
    rows_d, chan, rows_e = ing.shape[3], ing.shape[4], swapped[0].shape[2]
    return pl.pallas_call(
        functools.partial(exit_kernel, dims),
        in_specs=[pl.BlockSpec(memory_space=pltpu.SMEM)] + [vmem_spec()] * 2 + [any_spec()] * 6 + [vmem_spec()] * 4,
        out_specs=[vmem_spec()] * 2 + [any_spec()] * 6,
        out_shape=[
            shape((MBLK, D), BF16), shape((8, 128), F32), shape((MODES, rows_d, INNER), BF16),
            *[shape((nl - 1, MODES) + part.shape[2:], F32) for part in swapped],
            *[shape((nl - 1, part.shape[-2], rows_e), F32) for part in rest],
        ],
        scratch_shapes=[
            VMEM((ns // NX, NX, ny, MBLK, D), BF16),
            VMEM((D // 128, 8, 128), F32), VMEM((devices, 8, 128), F32), VMEM((groups, MODES, rows_d, chan), BF16),
            DMA((nl, 5, 2)), DMA((devices, 2)), DMA((groups, 2)),
            *column_scratch(dims, rows_d, chan),
            *reduce_scratch(dims, MBLK, D, BF16),
        ],
        compiler_params=comm_params(4, 63),
        cost_estimate=comm_cost(100),
        name="leave",
    )(modes, joint, w_in, ing, *swapped, *rest, x, cot, gain, pick)


def body(
    tokens, modality, cotangent, in_weight, x_weight, dt_weight, out_weight, norm_gain, channel_params,
    in_first, in_second, x_first, x_second, dt_first, dt_second, out_first, out_second,
    gain_first, gain_second, chan_first, chan_second,
):
    nb, seqs, los = lax.axis_size("seq"), lax.axis_size("hi"), lax.axis_size("lo")
    dims = (nb, seqs, los)
    groups = nb * seqs
    chan = INNER // groups
    rows_d = in_weight.shape[0]
    rows_e = x_weight.shape[0]
    plan = Plan(nb, seqs, chan)
    low = lax.axis_index("lo")
    index = (lax.axis_index("seq") * seqs + lax.axis_index("hi")) * los + low
    lane = lax.rem(index * rows_d, 128)

    mode_here = modality[0, 0]
    small = jnp.zeros((8, 128), F32)
    small = lax.dynamic_update_slice(small, rounded(norm_gain.T), (0, lane))
    small = small.at[MODES].set(mode_here.astype(F32))
    pick = (mode_here == lax.broadcasted_iota(jnp.int32, (8, 128), 0)).astype(F32)

    in_cols = in_weight.astype(BF16).swapaxes(0, 1)
    x_low = x_weight.astype(BF16).transpose(1, 2, 0).reshape(MODES * XCOLS, rows_e)
    dt_low = dt_weight.astype(BF16).swapaxes(0, 1)
    out_low = out_weight.astype(BF16).swapaxes(0, 1)
    chan_low = jnp.pad(rounded(channel_params).T, ((0, PAR_ROWS - channel_params.shape[1]), (0, 0)))
    mode_row, gain, normal, w_in, w_dt, w_out, w_x, par = entry(
        dims, small, pick, tokens[0], in_cols, dt_low, out_low, x_low, chan_low
    )
    modes = mode_row[0, :groups].astype(jnp.int32)
    w_x = lanes_join(w_x).reshape(MODES, XCOLS, chan)
    par = lanes_join(par)
    rates = -jnp.exp(par[PAR_RATES : PAR_RATES + STATE])
    rates_f = plan.fold_rates(rates / LN2)
    select = jnp.asarray(plan.select(), BF16)

    cot_here, _ = lax.optimization_barrier((cotangent[0], gain))
    cot = lax.all_gather(cot_here, GROUP, axis=0)

    inner, gate, pre, act, proj_part = front(plan, modes, normal, w_in, w_x, par)
    (proj,) = share(dims, 2, proj_part)
    proj = proj.reshape(groups, XCOLS, MBLK)
    spot = jnp.stack([lax.axis_index("seq") % NX, lax.axis_index("hi")]).astype(jnp.int32)
    scanned, mixed, before, last, *out_parts = forward_scan(
        plan, jnp.concatenate([modes, spot]), proj, act, gate, w_dt, w_out, par, rates_f, select
    )
    staged = Staged(dims, out_parts)
    crossed = staged.plane()

    bact, bgate, bproj_part, dt_g, out_g, gate_g, sums_a = backward_scan(
        plan, modes, cot, normal, proj, act, gate, scanned, mixed, before, last, w_dt, w_out, par, rates_f, select
    )
    dt_g = dt_g.reshape(MODES, los, rows_e, RANK)
    out_g = out_g.reshape(MODES, los, rows_e, D)
    gate_g = gate_g.reshape(MODES, groups, los, rows_d, chan)
    crossed, bproj_part = lax.optimization_barrier((crossed, bproj_part))
    bproj, gate_ready = share(dims, 3, bproj_part, (gate_g,))
    bproj = bproj.reshape(groups, XCOLS, MBLK)
    gate_grad = lax.all_to_all(gate_ready, GROUP, 0, 0)
    joint, in_g, x_g, sums_b = tail(
        plan, modes, bproj, bact, bgate, pre, act, inner, normal, w_x, par
    )
    rest = (x_g.reshape(MODES * XCOLS, chan), sums_a, sums_b)
    input_grad, gain_sum, inner_grad, dt_far, out_far, *rest_far = leave(
        dims, modes, joint, w_in, in_g.reshape(MODES, groups, los, rows_d, chan), (dt_g, out_g),
        tuple(lanes_split(part, los) for part in rest), tokens[0], cotangent[0], gain, pick,
    )

    crossed, gain_sum = lax.optimization_barrier((crossed, gain_sum))
    pieces = staged.along(staged.line(crossed))

    def merged(near, far):
        return lax.dynamic_index_in_dim(near, low, 1, keepdims=False) + jnp.sum(far, 0)

    gate_grad = gate_grad.transpose(2, 1, 0, 3).reshape(rows_d, MODES, INNER)
    in_grad = jnp.concatenate([inner_grad.swapaxes(0, 1), gate_grad], 2).astype(F32)
    dt_grad = merged(dt_g, dt_far).swapaxes(0, 1)
    out_grad = merged(out_g, out_far).swapaxes(0, 1)
    x_sum, sum_a, sum_b = (
        lax.dynamic_slice_in_dim(near, low * rows_e, rows_e, 1) + jnp.sum(far, 0) for near, far in zip(rest, rest_far)
    )
    x_grad = x_sum.reshape(MODES, XCOLS, rows_e).transpose(2, 0, 1)
    chan_grad = jnp.concatenate(
        [
            sum_a[:MODES],
            sum_b[CONV : CONV + 1],
            sum_a[MODES : MODES + 1],
            sum_b[:CONV],
            sum_a[SUM_LOG:],
        ],
        0,
    ).T
    gain_grad = lax.dynamic_slice(gain_sum, (0, lane), (MODES, rows_d)).T

    in_new = adam_update(in_weight, in_first, in_second, in_grad, D ** (-0.5))
    x_new = adam_update(x_weight, x_first, x_second, x_grad, INNER ** (-0.5))
    dt_new = adam_update(dt_weight, dt_first, dt_second, dt_grad, RANK ** (-0.5))
    out_new = adam_update(out_weight, out_first, out_second, out_grad, (4 * INNER) ** (-0.5))
    gain_new = adam_update(norm_gain, gain_first, gain_second, gain_grad, SMALL_RATE)
    chan_new = adam_update(channel_params, chan_first, chan_second, chan_grad, CHAN_RATE)
    pieces, in_new = lax.optimization_barrier((pieces, in_new))
    out_sum = tokens[0].astype(F32)
    for piece in pieces:
        out_sum = out_sum + piece.astype(F32)
    block_out = out_sum.astype(BF16)[None]
    return (
        block_out,
        input_grad[None],
        *in_new,
        in_new[0].astype(BF16),
        *x_new,
        x_new[0].astype(BF16),
        *dt_new,
        dt_new[0].astype(BF16),
        *out_new,
        out_new[0].astype(BF16),
        *gain_new,
        *chan_new,
    )


def solution(mesh):
    seq, batch = mesh.shape["seq"], mesh.shape["batch"]
    high = max(1, min(batch, GROUPS // seq))
    split = Mesh(mesh.devices.reshape(seq, high, batch // high), EVERY)
    token = P(("hi", "lo"), "seq", None)
    wide = P(EVERY, None, None)
    flat = P(EVERY, None)
    return jax.shard_map(
        body,
        mesh=split,
        in_specs=(token, P(("hi", "lo"), "seq"), token) + (wide,) * 4 + (flat,) * 2 + (wide,) * 8 + (flat,) * 4,
        out_specs=(token,) * 2 + (wide,) * 16 + (flat,) * 6,
        check_vma=False,
    )
```

```python
import functools

import jax
import jax.numpy as jnp
import numpy as np
from jax import lax
from jax.experimental import pallas as pl
from jax.experimental.pallas import tpu as pltpu
from jax.sharding import Mesh
from jax.sharding import PartitionSpec as P

D = 2048
INNER = 4096
STATE = 16
CONV = 4
RANK = 128
MODES = 3
MBLK = 128
STEP = 5
XCOLS = RANK + 2 * STATE
GROUPS = 16

NORM_EPS = 1e-05
BETA_ONE = 0.5
BETA_TWO = 0.75
ADAM_EPS = 1e-08
DECAY = 0.01
SMALL_RATE = 0.1
CHAN_RATE = 2.0
LN2 = 0.6931471805599453
F32 = jnp.float32
BF16 = jnp.bfloat16

EVERY = ("seq", "hi", "lo")
GROUP = ("seq", "hi")
VMEM = pltpu.VMEM
MIB = 1024 * 1024


def adam_update(weight, first, second, grad, rate):
    first_new = BETA_ONE * first + (1.0 - BETA_ONE) * grad
    second_new = BETA_TWO * second + (1.0 - BETA_TWO) * grad * grad
    first_hat = first_new / (1.0 - BETA_ONE**STEP)
    second_hat = second_new / (1.0 - BETA_TWO**STEP)
    weight_new = weight - rate * (first_hat / (jnp.sqrt(second_hat) + ADAM_EPS) + DECAY * weight)
    return (weight_new, first_new, second_new)


def nt_dot(left, right):
    return lax.dot_general(left, right, (((1,), (1,)), ((), ())), preferred_element_type=F32)


def tn_dot(left, right):
    return lax.dot_general(left, right, (((0,), (0,)), ((), ())), preferred_element_type=F32)


def nn_dot(left, right):
    return jnp.dot(left, right, preferred_element_type=F32)


def add_outer(total_ref, mode, x_ref, q, right):
    piece = 512
    for k in range(D // piece):
        at = slice(k * piece, (k + 1) * piece)
        total_ref[mode, at, :] += tn_dot(x_ref[q, :, at], right)


def sigmoid(v):
    return 1.0 / (1.0 + jnp.exp(-v))


def rounded(v):
    return lax.reduce_precision(v, 8, 7)


def softplus(v):
    return jnp.maximum(v, 0.0) + jnp.log1p(jnp.exp(-jnp.abs(v)))


class Plan:
    def __init__(self, blocks, seqs, channels):
        self.nb = blocks
        self.seqs = seqs
        self.chan = channels
        self.halves = channels // 128
        self.fold = 8 // self.seqs
        self.groups = STATE // self.fold
        self.held = self.groups * self.halves

    def sub(self, f, q):
        return f * self.seqs + q

    def select(self):
        out = np.zeros((self.fold, 2 * STATE, 128), np.float32)
        for f in range(self.fold):
            for g in range(self.groups):
                out[f, g * self.fold + f, g] = 1.0
                out[f, STATE + g * self.fold + f, self.groups + g] = 1.0
        return out

    def summers(self):
        entry = np.zeros((self.groups * 128, 128), np.float32)
        leave = np.zeros((self.groups * 128, 128), np.float32)
        for g in range(self.groups):
            entry[g * 128 : (g + 1) * 128, g] = 1.0
            leave[g * 128 : (g + 1) * 128, self.groups + g] = 1.0
        return entry, leave

    def fold_rates(self, rates):
        shaped = rates.reshape(self.groups, self.fold, 1, self.halves, 128).transpose(3, 0, 1, 2, 4)
        wide = jnp.broadcast_to(shaped, (self.halves, self.groups, self.fold, self.seqs, 128))
        return wide.reshape(self.held, 8, 128)


NX = 2

PAR_SBIAS = 0
PAR_CBIAS = MODES
PAR_SKIP = MODES + 1
PAR_TAPS = MODES + 2
PAR_RATES = MODES + 2 + CONV
PAR_ROWS = 32
SUM_LOG = 8


def params_of(shape_like):
    return pltpu.CompilerParams(vmem_limit_bytes=shape_like * MIB)


def whole(shape):
    return pl.BlockSpec(shape, lambda *_: (0,) * len(shape), pipeline_mode=pl.Buffered(1))


def kept(shape):
    return pl.BlockSpec(shape, lambda *_: (0,) * len(shape))


def packed(index, seqs):
    return pl.BlockSpec((seqs, XCOLS, MBLK), index)


def packed_shape(blocks, kind=BF16):
    return jax.ShapeDtypeStruct((blocks, XCOLS, MBLK), kind)


def front_kernel(
    plan, modes, x_ref, w_ref, wx_ref, par_ref, inner_ref, gate_ref, pre_ref, act_ref, proj_ref, halo
):
    j = pl.program_id(0)
    channels = plan.chan

    @pl.when(j == 0)
    def _():
        halo[...] = jnp.zeros_like(halo)

    for q in range(plan.seqs):
        mode = modes[j * plan.seqs + q]
        joint = nn_dot(x_ref[q], w_ref[mode])
        inner_low = joint[:, :channels].astype(BF16)
        gate_ref[q] = joint[:, channels:]
        inner_ref[q] = inner_low
        inner = inner_low.astype(F32)
        wide = jnp.concatenate([halo[q], inner], 0)
        halo[q] = inner[MBLK - 8 :]
        pre = par_ref[PAR_CBIAS : PAR_CBIAS + 1, :]
        for k in range(CONV):
            pre = pre + par_ref[PAR_TAPS + k : PAR_TAPS + k + 1, :] * wide[5 + k : 5 + k + MBLK]
        pre_ref[q] = pre
        act_low = (pre * sigmoid(pre)).astype(BF16)
        act_ref[q] = act_low
        proj_ref[q, :MBLK] = nt_dot(act_low, wx_ref[mode, :RANK]).astype(BF16)
        proj_ref[q, MBLK:] = nt_dot(wx_ref[mode, RANK:], act_low).astype(BF16)


def front(plan, modes, normal, w_in, w_x, par):
    nb, seqs, chan = plan.nb, plan.seqs, plan.chan

    def rows(width):
        return pl.BlockSpec((seqs, MBLK, width), lambda j, *_: (j, 0, 0))

    def out(width, kind):
        return jax.ShapeDtypeStruct((nb * seqs, MBLK, width), kind)

    return pl.pallas_call(
        functools.partial(front_kernel, plan),
        grid_spec=pltpu.PrefetchScalarGridSpec(
            num_scalar_prefetch=1,
            grid=(nb,),
            in_specs=[rows(D), whole(w_in.shape), whole(w_x.shape), whole(par.shape)],
            out_specs=[rows(chan), rows(chan), rows(chan), rows(chan), packed(lambda j, *_: (j, 0, 0), seqs)],
            scratch_shapes=[VMEM((seqs, 8, chan), F32)],
        ),
        out_shape=[out(chan, BF16), out(chan, F32), out(chan, F32), out(chan, BF16), packed_shape(nb * seqs)],
        compiler_params=params_of(60),
        cost_estimate=pl.CostEstimate(
            flops=2 * nb * seqs * MBLK * D * 2 * chan, bytes_accessed=24 * MIB, transcendentals=0
        ),
        name="front",
    )(modes, normal, w_in, w_x, par)


def step_inputs(plan, mode, proj, wdt_ref, par_ref):
    rank_low = proj[:MBLK]
    raw = nt_dot(rank_low, wdt_ref[mode])
    biased = raw + par_ref[pl.ds(PAR_SBIAS + mode, 1), :]
    return rank_low, biased


def scan_kernel(
    plan, modes, proj_ref, act_ref, gate_ref, wdt_ref, wout_ref, par_ref, rates_ref, sel_ref,
    scanned_ref, mixed_ref, before_ref, last_ref, *refs,
):
    part_refs, (st, dr, el, yy, state) = refs[:-5], refs[-5:]
    j = pl.program_id(0)
    groups = plan.groups
    count = plan.nb * plan.seqs
    here_x, here_y = modes[count], modes[count + 1]

    @pl.when(j == 0)
    def _():
        state[...] = jnp.zeros_like(state)

    for q in range(plan.seqs):
        mode = modes[j * plan.seqs + q]
        proj = proj_ref[q]
        _, biased = step_inputs(plan, mode, proj, wdt_ref, par_ref)
        steps = softplus(biased)
        drive = steps * act_ref[q].astype(F32)
        for f in range(plan.fold):
            at = pl.ds(plan.sub(f, q), MBLK, stride=8)
            el[at, :] = tn_dot(proj[MBLK:], sel_ref[f])
            for c in range(plan.halves):
                st[c, at, :] = steps[:, c * 128 : (c + 1) * 128]
                dr[c, at, :] = drive[:, c * 128 : (c + 1) * 128]

    unroll = 16

    def some_steps(i, carry):
        now = list(carry)
        for u in range(unroll):
            t = i * unroll + u
            rows = pl.ds(pl.multiple_of(t * 8, 8), 8)
            pair = el[rows, :]
            entry = [jnp.broadcast_to(pair[:, g : g + 1], (8, 128)) for g in range(groups)]
            leave = [jnp.broadcast_to(pair[:, groups + g : groups + g + 1], (8, 128)) for g in range(groups)]
            for c in range(plan.halves):
                step = st[c, rows, :]
                drive = dr[c, rows, :]
                total = None
                for g in range(groups):
                    v = c * groups + g
                    before_ref[t, v] = now[v]
                    now[v] = jnp.exp2(step * rates_ref[v]) * now[v] + drive * entry[g]
                    term = now[v] * leave[g]
                    total = term if total is None else total + term
                yy[c, rows, :] = total
        return tuple(now)

    final = lax.fori_loop(0, MBLK // unroll, some_steps, tuple(state[v] for v in range(plan.held)))
    for v in range(plan.held):
        state[v] = final[v]
        last_ref[v] = final[v]

    skip = par_ref[PAR_SKIP : PAR_SKIP + 1, :]
    for q in range(plan.seqs):
        mode = modes[j * plan.seqs + q]
        parts = []
        for c in range(plan.halves):
            total = yy[c, pl.ds(plan.sub(0, q), MBLK, stride=8), :]
            for f in range(1, plan.fold):
                total = total + yy[c, pl.ds(plan.sub(f, q), MBLK, stride=8), :]
            parts.append(total)
        scanned = parts[0] if len(parts) == 1 else jnp.concatenate(parts, 1)
        scanned_ref[q] = scanned
        gate = gate_ref[q]
        mixed = ((scanned + skip * act_ref[q].astype(F32)) * (gate * sigmoid(gate))).astype(BF16)
        mixed_ref[q] = mixed
        dx = lax.rem(lax.rem(j, NX) + here_x, NX)
        dy = lax.rem(q + here_y, plan.seqs)
        product = nn_dot(mixed, wout_ref[mode]).astype(BF16)
        for r, part_ref in enumerate(part_refs):

            @pl.when(dx * plan.seqs + dy == r)
            def _():
                part_ref[0] = product


def forward_scan(plan, modes, proj, act, gate, w_dt, w_out, par, rates, select):
    nb, seqs, chan, held = plan.nb, plan.seqs, plan.chan, plan.held
    halves = VMEM((plan.halves, MBLK * 8, 128), F32)
    plane = NX * seqs

    def rows(width):
        return pl.BlockSpec((seqs, MBLK, width), lambda j, *_: (j, 0, 0))

    def out(width, kind):
        return jax.ShapeDtypeStruct((nb * seqs, MBLK, width), kind)

    return pl.pallas_call(
        functools.partial(scan_kernel, plan),
        grid_spec=pltpu.PrefetchScalarGridSpec(
            num_scalar_prefetch=1,
            grid=(nb,),
            in_specs=[
                packed(lambda j, *_: (j, 0, 0), seqs), rows(chan), rows(chan), whole(w_dt.shape), whole(w_out.shape),
                whole(par.shape), whole(rates.shape), whole(select.shape),
            ],
            out_specs=[
                rows(chan), rows(chan),
                pl.BlockSpec((MBLK, held, 8, 128), lambda j, *_: (j, 0, 0, 0)),
                kept((held, 8, 128)),
                *[pl.BlockSpec((1, MBLK, D), lambda j, *_: (j // NX, 0, 0))] * plane,
            ],
            scratch_shapes=[halves, halves, VMEM((MBLK * 8, 128), F32), halves, VMEM((held, 8, 128), F32)],
        ),
        out_shape=[
            out(chan, F32), out(chan, BF16),
            jax.ShapeDtypeStruct((nb * MBLK, held, 8, 128), F32),
            jax.ShapeDtypeStruct((held, 8, 128), F32),
            *[jax.ShapeDtypeStruct((nb // NX, MBLK, D), BF16)] * plane,
        ],
        compiler_params=params_of(60),
        cost_estimate=pl.CostEstimate(
            flops=60 * nb * MBLK * held * 1024, bytes_accessed=150 * MIB, transcendentals=nb * MBLK * held * 1024
        ),
        name="forward_scan",
    )(modes, proj, act, gate, w_dt, w_out, par, rates, select)


def back_kernel(
    plan, modes, cot_ref, x_ref, proj_ref, act_ref, gate_ref, scanned_ref, mixed_ref, before_ref, last_ref,
    wdt_ref, wout_ref, par_ref, rates_ref, sel_ref, sume_ref, suml_ref,
    bact_ref, bgate_ref, bproj_ref, dtg_ref, outg_ref, ing_ref, sums_ref,
    logr_ref, st, dr, el, bs, aa, uu, pe, plv, carry_ref, after_ref,
):
    i = pl.program_id(0)
    j = plan.nb - 1 - i
    groups = plan.groups

    @pl.when(i == 0)
    def _():
        carry_ref[...] = jnp.zeros_like(carry_ref)
        after_ref[...] = last_ref[...]
        dtg_ref[...] = jnp.zeros_like(dtg_ref)
        outg_ref[...] = jnp.zeros_like(outg_ref)
        ing_ref[...] = jnp.zeros_like(ing_ref)
        sums_ref[...] = jnp.zeros_like(sums_ref)
        logr_ref[...] = jnp.zeros_like(logr_ref)

    skip = par_ref[PAR_SKIP : PAR_SKIP + 1, :]
    held = []
    for q in range(plan.seqs):
        mode = modes[j * plan.seqs + q]
        proj = proj_ref[q]
        rank_low, biased = step_inputs(plan, mode, proj, wdt_ref, par_ref)
        steps = softplus(biased)
        act = act_ref[q].astype(F32)
        drive = steps * act
        back_mixed = nt_dot(cot_ref[q], wout_ref[mode])
        gate = gate_ref[q]
        sig = sigmoid(gate)
        back_scanned = back_mixed * (gate * sig)
        slope = sig * (1.0 + gate * (1.0 - sig))
        back_gate = (back_mixed * (scanned_ref[q] + skip * act) * slope).astype(BF16)
        bgate_ref[q] = back_gate
        add_outer(ing_ref, mode, x_ref, q, back_gate)
        outg_ref[mode] += tn_dot(mixed_ref[q], cot_ref[q])
        for f in range(plan.fold):
            at = pl.ds(plan.sub(f, q), MBLK, stride=8)
            el[at, :] = tn_dot(proj[MBLK:], sel_ref[f])
            for c in range(plan.halves):
                cols = slice(c * 128, (c + 1) * 128)
                st[c, at, :] = steps[:, cols]
                dr[c, at, :] = drive[:, cols]
                bs[c, at, :] = back_scanned[:, cols]
        held.append((mode, rank_low, biased, steps, act, back_scanned))

    unroll = 16

    def some_steps(i, carry):
        lam_in = list(carry[0])
        after = list(carry[1])
        log_sum = list(carry[2])
        for u in range(unroll):
            t = MBLK - 1 - (i * unroll + u)
            rows = pl.ds(pl.multiple_of(t * 8, 8), 8)
            pair = el[rows, :]
            entry = [jnp.broadcast_to(pair[:, g : g + 1], (8, 128)) for g in range(groups)]
            leave = [jnp.broadcast_to(pair[:, groups + g : groups + g + 1], (8, 128)) for g in range(groups)]
            entry_sum, leave_sum = [None] * groups, [None] * groups
            for c in range(plan.halves):
                step = st[c, rows, :]
                drive = dr[c, rows, :]
                push = bs[c, rows, :]
                a_sum = None
                u_sum = None
                for g in range(groups):
                    v = c * groups + g
                    rate = rates_ref[v]
                    before = before_ref[t, v]
                    lam = push * leave[g] + lam_in[v]
                    leave_term = push * after[v]
                    entry_term = lam * drive
                    leave_sum[g] = leave_term if c == 0 else leave_sum[g] + leave_term
                    entry_sum[g] = entry_term if c == 0 else entry_sum[g] + entry_term
                    moved = lam * jnp.exp2(step * rate)
                    lam_in[v] = moved
                    after[v] = before
                    felt = moved * before
                    a_term = rate * felt
                    u_term = lam * entry[g]
                    a_sum = a_term if a_sum is None else a_sum + a_term
                    u_sum = u_term if u_sum is None else u_sum + u_term
                    log_sum[v] = log_sum[v] + step * felt
                aa[c, rows, :] = a_sum
                uu[c, rows, :] = u_sum
            for g in range(groups):
                cols = slice(g * 128, (g + 1) * 128)
                pe[rows, cols] = entry_sum[g]
                plv[rows, cols] = leave_sum[g]
        return (tuple(lam_in), tuple(after), tuple(log_sum))

    start = (
        tuple(carry_ref[v] for v in range(plan.held)),
        tuple(after_ref[v] for v in range(plan.held)),
        tuple(logr_ref[v] for v in range(plan.held)),
    )
    lam_end, after_end, log_end = lax.fori_loop(0, MBLK // unroll, some_steps, start)
    for v in range(plan.held):
        carry_ref[v] = lam_end[v]
        after_ref[v] = after_end[v]
        logr_ref[v] = log_end[v]

    el[...] = nn_dot(pe[...].astype(BF16), sume_ref[...]) + nn_dot(plv[...].astype(BF16), suml_ref[...])

    for q in range(plan.seqs):
        mode, rank_low, biased, steps, act, back_scanned = held[q]
        a_parts, u_parts = [], []
        back_pair = jnp.zeros((2 * STATE, MBLK), F32)
        for c in range(plan.halves):
            a_total, u_total = None, None
            for f in range(plan.fold):
                at = pl.ds(plan.sub(f, q), MBLK, stride=8)
                a_term, u_term = aa[c, at, :], uu[c, at, :]
                a_total = a_term if a_total is None else a_total + a_term
                u_total = u_term if u_total is None else u_total + u_term
            a_parts.append(a_total * LN2)
            u_parts.append(u_total)
        for f in range(plan.fold):
            both = el[pl.ds(plan.sub(f, q), MBLK, stride=8), :]
            back_pair = back_pair + nt_dot(sel_ref[f], both.astype(BF16))
        a_all = a_parts[0] if len(a_parts) == 1 else jnp.concatenate(a_parts, 1)
        u_all = u_parts[0] if len(u_parts) == 1 else jnp.concatenate(u_parts, 1)
        back_steps = a_all + act * u_all
        bact_ref[q] = skip * back_scanned + steps * u_all
        back_pre_step = back_steps * sigmoid(biased)
        raw_low = back_pre_step.astype(BF16)
        bproj_ref[q, :MBLK] = nn_dot(raw_low, wdt_ref[mode]).astype(BF16)
        bproj_ref[q, MBLK:] = back_pair.astype(BF16)
        dtg_ref[mode] += tn_dot(raw_low, rank_low)
        sums_ref[pl.ds(mode, 1), :] += jnp.sum(back_pre_step, 0, keepdims=True)
        sums_ref[MODES : MODES + 1, :] += jnp.sum(back_scanned * act, 0, keepdims=True)

    @pl.when(j == 0)
    def _():
        for v in range(plan.held):
            c, g = v // groups, v % groups
            for f in range(plan.fold):
                at = plan.sub(f, 0)
                total = jnp.sum(logr_ref[v, at : at + plan.seqs, :], 0, keepdims=True)
                n = SUM_LOG + g * plan.fold + f
                scaled = total * rates_ref[v, at : at + 1, :] * LN2
                sums_ref[n : n + 1, c * 128 : (c + 1) * 128] = scaled


def backward_scan(plan, modes, cot, normal, proj, act, gate, scanned, mixed, before, last, w_dt, w_out, par, rates, select):
    nb, seqs, chan, groups, held = plan.nb, plan.seqs, plan.chan, plan.groups, plan.held
    sum_entry, sum_leave = plan.summers()
    sum_entry, sum_leave = jnp.asarray(sum_entry, BF16), jnp.asarray(sum_leave, BF16)

    def rows(width):
        return pl.BlockSpec((seqs, MBLK, width), lambda i, *_: (nb - 1 - i, 0, 0))

    def out(width, kind):
        return jax.ShapeDtypeStruct((nb * seqs, MBLK, width), kind)

    tall = VMEM((plan.halves, MBLK * 8, 128), F32)
    return pl.pallas_call(
        functools.partial(back_kernel, plan),
        grid_spec=pltpu.PrefetchScalarGridSpec(
            num_scalar_prefetch=1,
            grid=(nb,),
            in_specs=[
                rows(D), rows(D), packed(lambda i, *_: (nb - 1 - i, 0, 0), seqs),
                rows(chan), rows(chan), rows(chan), rows(chan),
                pl.BlockSpec((MBLK, held, 8, 128), lambda i, *_: (nb - 1 - i, 0, 0, 0)),
                whole(last.shape), whole(w_dt.shape), whole(w_out.shape), whole(par.shape),
                whole(rates.shape), whole(select.shape),
                whole(sum_entry.shape), whole(sum_leave.shape),
            ],
            out_specs=[
                rows(chan), rows(chan), packed(lambda i, *_: (nb - 1 - i, 0, 0), seqs),
                kept((MODES, chan, RANK)), kept((MODES, chan, D)), kept((MODES, D, chan)),
                kept((SUM_LOG + STATE, chan)),
            ],
            scratch_shapes=[
                VMEM((held, 8, 128), F32), tall, tall, VMEM((MBLK * 8, 128), F32), tall, tall, tall,
                VMEM((MBLK * 8, groups * 128), F32), VMEM((MBLK * 8, groups * 128), F32),
                VMEM((held, 8, 128), F32), VMEM((held, 8, 128), F32),
            ],
        ),
        out_shape=[
            out(chan, F32), out(chan, BF16), packed_shape(nb * seqs),
            jax.ShapeDtypeStruct((MODES, chan, RANK), F32),
            jax.ShapeDtypeStruct((MODES, chan, D), F32),
            jax.ShapeDtypeStruct((MODES, D, chan), F32),
            jax.ShapeDtypeStruct((SUM_LOG + STATE, chan), F32),
        ],
        compiler_params=params_of(60),
        cost_estimate=pl.CostEstimate(
            flops=100 * nb * MBLK * held * 1024, bytes_accessed=300 * MIB, transcendentals=nb * MBLK * held * 1024
        ),
        name="backward_scan",
    )(modes, cot, normal, proj, act, gate, scanned, mixed, before, last, w_dt, w_out, par, rates, select,
      sum_entry, sum_leave)


def tail_kernel(
    plan, modes, bp_ref, bact_ref, bgate_ref, pre_ref, act_ref, inner_ref, earlier_ref, x_ref,
    wx_ref, par_ref,
    joint_ref, ing_ref, xg_ref, sums_ref,
    halo,
):
    i = pl.program_id(0)
    j = plan.nb - 1 - i
    channels = plan.chan

    @pl.when(i == 0)
    def _():
        halo[...] = jnp.zeros_like(halo)
        ing_ref[...] = jnp.zeros_like(ing_ref)
        xg_ref[...] = jnp.zeros_like(xg_ref)
        sums_ref[...] = jnp.zeros_like(sums_ref)

    first = jnp.where(j == 0, 0.0, 1.0)
    for q in range(plan.seqs):
        mode = modes[j * plan.seqs + q]
        rank_low, pair_low = bp_ref[q, :MBLK], bp_ref[q, MBLK:]
        back_act = bact_ref[q] + nn_dot(rank_low, wx_ref[mode, :RANK]) + tn_dot(pair_low, wx_ref[mode, RANK:])
        xg_ref[mode, :RANK] += tn_dot(rank_low, act_ref[q])
        xg_ref[mode, RANK:] += nn_dot(pair_low, act_ref[q])
        pre = pre_ref[q]
        sig = sigmoid(pre)
        back_pre = back_act * (sig * (1.0 + pre * (1.0 - sig)))
        wide = jnp.concatenate([back_pre, halo[q]], 0)
        halo[q] = back_pre[:8]
        inner_wide = jnp.concatenate(
            [earlier_ref[q][MBLK - 16 :].astype(F32) * first, inner_ref[q].astype(F32)], 0
        )
        back_inner = None
        for k in range(CONV):
            term = par_ref[PAR_TAPS + k : PAR_TAPS + k + 1, :] * wide[CONV - 1 - k : CONV - 1 - k + MBLK]
            back_inner = term if back_inner is None else back_inner + term
            felt = back_pre * inner_wide[13 + k : 13 + k + MBLK]
            sums_ref[k : k + 1, :] += jnp.sum(felt, 0, keepdims=True)
        sums_ref[CONV : CONV + 1, :] += jnp.sum(back_pre, 0, keepdims=True)
        inner_low = back_inner.astype(BF16)
        joint_low = jnp.concatenate([inner_low, bgate_ref[q]], 1)
        joint_ref[q] = joint_low
        add_outer(ing_ref, mode, x_ref, q, inner_low)


def tail(plan, modes, bp, bact, bgate, pre, act, inner, normal, w_x, par):
    nb, seqs, chan = plan.nb, plan.seqs, plan.chan

    def rows(width):
        return pl.BlockSpec((seqs, MBLK, width), lambda i, *_: (nb - 1 - i, 0, 0))

    return pl.pallas_call(
        functools.partial(tail_kernel, plan),
        grid_spec=pltpu.PrefetchScalarGridSpec(
            num_scalar_prefetch=1,
            grid=(nb,),
            in_specs=[
                packed(lambda i, *_: (nb - 1 - i, 0, 0), seqs), rows(chan), rows(chan), rows(chan), rows(chan), rows(chan),
                pl.BlockSpec((seqs, MBLK, chan), lambda i, *_: (jnp.maximum(nb - 2 - i, 0), 0, 0)),
                rows(D), whole(w_x.shape), whole(par.shape),
            ],
            out_specs=[
                rows(2 * chan), kept((MODES, D, chan)), kept((MODES, XCOLS, chan)),
                kept((8, chan)),
            ],
            scratch_shapes=[VMEM((seqs, 8, chan), F32)],
        ),
        out_shape=[
            jax.ShapeDtypeStruct((nb * seqs, MBLK, 2 * chan), BF16),
            jax.ShapeDtypeStruct((MODES, D, chan), F32),
            jax.ShapeDtypeStruct((MODES, XCOLS, chan), F32),
            jax.ShapeDtypeStruct((8, chan), F32),
        ],
        compiler_params=params_of(60),
        cost_estimate=pl.CostEstimate(
            flops=4 * nb * seqs * MBLK * D * 2 * chan, bytes_accessed=40 * MIB, transcendentals=0
        ),
        name="tail",
    )(modes, bp, bact, bgate, pre, act, inner, inner, normal, w_x, par)


ANY = pl.ANY
DMA = pltpu.SemaphoreType.DMA


def any_spec():
    return pl.BlockSpec(memory_space=ANY)


def vmem_spec():
    return pl.BlockSpec(memory_space=VMEM)


def remote(src, dst, send, recv, device):
    return pltpu.make_async_remote_copy(
        src_ref=src, dst_ref=dst, send_sem=send, recv_sem=recv, device_id=device,
        device_id_type=pl.DeviceIdType.MESH,
    )


class Place:
    def __init__(self, dims):
        self.ns, self.ny, self.nl = dims
        self.nz = self.ns // NX
        self.groups = self.ns * self.ny
        self.devices = self.groups * self.nl
        seq = lax.axis_index("seq")
        self.z, self.x = lax.div(seq, NX), lax.rem(seq, NX)
        self.y = lax.axis_index("hi")
        self.l = lax.axis_index("lo")
        self.g = seq * self.ny + self.y
        self.i = self.g * self.nl + self.l
        self.ox, self.oy = NX - 1 - self.x, self.ny - 1 - self.y

    def device(self, z, x, y, low):
        return (z * NX + x, y, low)

    def of_group(self, g, low):
        return (lax.div(g, self.ny), lax.rem(g, self.ny), low)

    def of_index(self, i):
        return self.of_group(lax.div(i, self.nl), lax.rem(i, self.nl))

    def group(self, z, x, y):
        return (z * NX + x) * self.ny + y

    def relative(self, n, sign):
        plane = NX * self.ny
        dz, rest = lax.div(n, plane), lax.rem(n, plane)
        dx, dy = lax.div(rest, self.ny), lax.rem(rest, self.ny)
        z = lax.rem(self.z + self.nz + sign * dz, self.nz)
        x = lax.rem(self.x + NX + sign * dx, NX)
        y = lax.rem(self.y + self.ny + sign * dy, self.ny)
        return self.group(z, x, y)

    def in_plane(self, z, r):
        x = lax.rem(self.x + lax.div(r, self.ny), NX)
        y = lax.rem(self.y + lax.rem(r, self.ny), self.ny)
        return self.group(z, x, y)

    def after(self, n):
        return self.relative(jnp.int32(n), 1)

    def before(self, n):
        return self.relative(jnp.int32(n), -1)

    def x_peer(self):
        return self.device(self.z, self.ox, self.y, self.l)

    def y_peer(self):
        return self.device(self.z, self.x, self.oy, self.l)

    def z_after(self, k):
        return lax.rem(self.z + k, self.nz)

    def z_before(self, k):
        return lax.rem(self.z + self.nz - k, self.nz)

    def z_peer(self, k):
        return self.device(self.z_after(k), self.x, self.y, self.l)

    def low_after(self, k):
        return lax.rem(self.l + k, self.nl)

    def low_before(self, k):
        return lax.rem(self.l + self.nl - k, self.nl)

    def low_peer(self, k):
        return self.device(self.z, self.x, self.y, self.low_after(k))


def lanes_shape(rows, parts, width):
    return (rows, parts * width) if width % 128 == 0 else (parts, rows, width)


def lanes_at(ref, part, width):
    if width % 128 == 0:
        return ref.at[:, pl.ds(pl.multiple_of(part * width, width), width)]
    return ref.at[part]


def lanes_join(array):
    return array if array.ndim == 2 else jnp.swapaxes(array, 0, 1).reshape(array.shape[1], -1)


def lanes_split(array, parts):
    width = array.shape[1] // parts
    return array if width % 128 == 0 else array.reshape(array.shape[0], parts, width).swapaxes(0, 1)


def greet_all(here):
    barrier = pltpu.get_barrier_semaphore()

    def greet(k, carry):
        peer = here.of_index(lax.rem(here.i + k, here.devices))
        pl.semaphore_signal(barrier, inc=1, device_id=peer, device_id_type=pl.DeviceIdType.MESH)
        return carry

    lax.fori_loop(1, here.devices, greet, 0)
    pl.semaphore_wait(barrier, here.devices - 1)


def greet_near(here, low_too):
    barrier = pltpu.get_barrier_semaphore()
    peers = [here.x_peer()]
    if here.ny > 1:
        peers.append(here.y_peer())
    peers += [here.z_peer(k) for k in range(1, here.nz)]
    if low_too:
        peers += [here.low_peer(k) for k in range(1, here.nl)]
    for peer in peers:
        pl.semaphore_signal(barrier, inc=1, device_id=peer, device_id_type=pl.DeviceIdType.MESH)
    pl.semaphore_wait(barrier, len(peers))


def gather_sems(dims):
    nz = dims[0] // NX
    return [DMA((1,))] + [DMA((nz, 2))] * 6


def in_line(dims):
    return dims[0] // NX <= 4


class Gather:
    def __init__(self, here, own, out, rows, sems, line):
        self.here, self.own, self.out, self.half, self.line = here, own, out, rows // 2, line
        self.local, self.up, self.down, self.xs, self.ys, self.fx, self.fy = sems

    def block(self, z, x, y):
        return self.out.at[self.here.group(z, x, y)]

    def mine(self, z):
        return self.block(z, self.here.x, self.here.y)

    def keep(self):
        return pltpu.make_async_copy(self.own, self.out.at[self.here.g], self.local.at[0])

    def next(self, src, dst, sems, d, step):
        here = self.here
        peer = here.device(here.z + step, here.x, here.y, here.l)
        return remote(src, dst, sems.at[d, 0], sems.at[d, 1], peer)

    def far(self, k):
        here = self.here
        return remote(self.own, self.out.at[here.g], self.up.at[k, 0], self.up.at[k, 1], here.z_peer(k))

    def cross(self, z, src):
        here = self.here
        dst = self.mine(z)
        out = [remote(src, dst, self.xs.at[z, 0], self.xs.at[z, 1], here.x_peer())]
        if here.ny > 1:
            out.append(remote(src, dst, self.ys.at[z, 0], self.ys.at[z, 1], here.y_peer()))
        return out

    def spread(self, z, src):
        for copy in self.cross(z, src):
            copy.start()

    def start(self):
        here = self.here
        self.keep().start()
        if self.line:
            at = self.out.at[here.g]

            @pl.when(here.z + 1 < here.nz)
            def _():
                self.next(self.own, at, self.up, 0, 1).start()

            @pl.when(here.z > 0)
            def _():
                self.next(self.own, at, self.down, 0, -1).start()

        else:
            for k in range(1, here.nz):
                self.far(k).start()
        self.spread(here.z, self.own)

    def step(self, d):
        here = self.here
        if not self.line:
            z = here.z_before(d)
            self.far(d).wait_recv()
            self.spread(z, self.mine(z))
            return
        for sems, sign in ((self.up, 1), (self.down, -1)):
            z = here.z - sign * d
            on = here.z + sign

            @pl.when((z >= 0) & (z < here.nz))
            def _():
                got = self.mine(z)
                self.next(got, got, sems, d - 1, -sign).wait_recv()

                @pl.when((on >= 0) & (on < here.nz))
                def _():
                    self.next(got, got, sems, d, sign).start()

                self.spread(z, got)

    def halves(self, z, first):
        here = self.here
        to_y = self.block(z, here.ox, here.y) if first else self.block(z, here.ox, here.oy)
        to_x = self.block(z, here.x, here.oy) if first else self.block(z, here.ox, here.oy)
        upper, lower = to_y.at[pl.ds(0, self.half)], to_x.at[pl.ds(self.half, self.half)]
        return (
            remote(upper, upper, self.fy.at[z, 0], self.fy.at[z, 1], here.y_peer()),
            remote(lower, lower, self.fx.at[z, 0], self.fx.at[z, 1], here.x_peer()),
        )

    def forward(self, z):
        here = self.here
        copies = self.cross(z, self.mine(z))
        copies[0].wait_recv()
        if here.ny > 1:
            to_y, to_x = self.halves(z, True)
            to_y.start()
            copies[1].wait_recv()
            to_x.start()

    def forward_all(self):
        here = self.here
        self.forward(here.z)
        for d in range(1, here.nz):
            if self.line:
                for z in (here.z - d, here.z + d):

                    @pl.when((z >= 0) & (z < here.nz))
                    def _():
                        self.forward(z)

            else:
                self.forward(here.z_before(d))

    def end(self):
        here = self.here
        self.keep().wait()

        def finish(z, carry):
            for copy in self.cross(z, self.mine(z)):
                copy.wait_send()
            if here.ny > 1:
                for copy in self.halves(z, False):
                    copy.wait()
            return carry

        lax.fori_loop(0, here.nz, finish, 0)
        if not self.line:
            for k in range(1, here.nz):
                self.far(k).wait_send()
            return
        for sems, sign in ((self.up, 1), (self.down, -1)):
            on = here.z + sign
            for d in range(here.nz):
                z = here.z - sign * d

                @pl.when((z >= 0) & (z < here.nz) & (on >= 0) & (on < here.nz))
                def _():
                    self.next(self.mine(z), self.mine(z), sems, d, sign).wait_send()


def reduce_scratch(dims, rows, width, kind):
    ns, ny, _ = dims
    nz = ns // NX
    ra = rows // 2 if ny > 1 else rows
    rb = rows // 2
    out = [
        VMEM((nz, ny, ra, width), kind), VMEM((rows, width), F32),
        VMEM((nz, rows, width), kind), VMEM((nz, rows, width), kind),
        VMEM((1, 16, 128), kind),
        DMA((nz, 2)), DMA((nz, 2)), DMA((nz, 2)), DMA((nz, 2)), DMA((nz, 2)), DMA((nz, 2)),
    ]
    if ny > 1:
        out += [VMEM((nz, NX, rb, width), kind)] + [VMEM((nz, rb, width), kind)] * 4
    return out


class Reduce:
    def __init__(self, here, part, rows, bufs, line):
        self.here, self.part, self.line = here, part, line
        self.r1a, self.acc, self.s3, self.r3, self.r3d = bufs[:5]
        self.s1, self.s1b, self.s2, self.s2b, self.up, self.down = bufs[5:11]
        self.two = here.ny > 1
        ra = rows // 2 if self.two else rows
        self.top, self.low = pl.ds(0, ra), pl.ds(ra, rows - ra)
        if self.two:
            self.r1b, self.t2a, self.r2a, self.t2b, self.r2b = bufs[11:]

    def target(self, k):
        if not self.line:
            return self.here.z_after(k + 1)
        k = jnp.int32(k)
        half = lax.div(k, 2)
        return jnp.where(lax.rem(k, 2) == 0, self.here.nz - 1 - half, half)

    def copies(self, k):
        here, part, z = self.here, self.part, self.target(k)
        out = [remote(part.at[z, here.ox, :, self.top], self.r1a.at[k], self.s1.at[k, 0], self.s1.at[k, 1], here.x_peer())]
        if self.two:
            out.append(
                remote(part.at[z, :, here.oy, self.low], self.r1b.at[k], self.s1b.at[k, 0], self.s1b.at[k, 1], here.y_peer())
            )
        return out

    def crossed(self, k):
        here = self.here
        return (
            remote(self.t2a.at[k], self.r2a.at[k], self.s2.at[k, 0], self.s2.at[k, 1], here.y_peer()),
            remote(self.t2b.at[k], self.r2b.at[k], self.s2b.at[k, 0], self.s2b.at[k, 1], here.x_peer()),
        )

    def first(self, k):
        for copy in self.copies(k):
            copy.start()

    def second(self, k):
        here, part, z = self.here, self.part, self.target(k)
        kind = part.dtype
        copies = self.copies(k)
        copies[0].wait_recv()
        if self.two:
            total = part[z, here.x, here.oy, self.top].astype(F32) + self.r1a[k, here.oy].astype(F32)
            self.t2a[k] = total.astype(kind)
            a, b = self.crossed(k)
            a.start()
            copies[1].wait_recv()
            total = part[z, here.ox, here.y, self.low].astype(F32) + self.r1b[k, here.ox].astype(F32)
            self.t2b[k] = total.astype(kind)
            b.start()

    def totals(self, k):
        here, part, z = self.here, self.part, self.target(k)
        out = [(self.top, part[z, here.x, here.y, self.top].astype(F32) + self.r1a[k, here.y].astype(F32))]
        if self.two:
            for copy in self.crossed(k):
                copy.wait_recv()
            lower = part[z, here.x, here.y, self.low].astype(F32) + self.r1b[k, here.x].astype(F32)
            out = [(self.top, out[0][1] + self.r2a[k].astype(F32)), (self.low, lower + self.r2b[k].astype(F32))]
        return out

    def flows(self):
        return ((self.up, self.r3, 1), (self.down, self.r3d, -1))

    def along(self, z, sems, slot, step):
        here = self.here
        peer = here.device(here.z + step, here.x, here.y, here.l)
        return remote(self.s3.at[z], slot.at[z], sems.at[z, 0], sems.at[z, 1], peer)

    def straight(self, k):
        return remote(self.s3.at[k], self.r3.at[k], self.up.at[k, 0], self.up.at[k, 1], self.here.z_peer(k + 1))

    def third(self, k):
        here = self.here
        kind = self.part.dtype
        z = self.target(k)
        if not self.line:
            for rows, total in self.totals(k):
                self.s3[k, rows] = total.astype(kind)
            self.straight(k).start()
            return

        @pl.when(z == here.z)
        def _():
            for rows, total in self.totals(k):
                self.acc[rows] = total

        for sems, slot, sign in self.flows():
            back = here.z - sign

            @pl.when(sign * (z - here.z) > 0)
            def _():
                totals = self.totals(k)

                @pl.when((back >= 0) & (back < here.nz))
                def _():
                    self.along(z, sems, slot, -sign).wait_recv()
                    for rows, total in totals:
                        self.s3[z, rows] = (total + slot[z, rows].astype(F32)).astype(kind)

                @pl.when((back < 0) | (back >= here.nz))
                def _():
                    for rows, total in totals:
                        self.s3[z, rows] = total.astype(kind)

                self.along(z, sems, slot, sign).start()

    def last(self):
        here = self.here
        if not self.line:
            for rows, total in self.totals(here.nz - 1):
                self.acc[rows] = total

            def add(k, carry):
                self.straight(k).wait_recv()
                self.acc[...] += self.r3[k].astype(F32)
                return carry

            lax.fori_loop(0, here.nz - 1, add, 0)
            return
        for sems, slot, sign in self.flows():
            back = here.z - sign

            @pl.when((back >= 0) & (back < here.nz))
            def _():
                self.along(here.z, sems, slot, -sign).wait_recv()
                self.acc[...] += slot[here.z].astype(F32)

    def end(self):
        here = self.here

        def finish(k, carry):
            for copy in self.copies(k):
                copy.wait_send()
            if self.two:
                for copy in self.crossed(k):
                    copy.wait_send()
            return carry

        lax.fori_loop(0, here.nz, finish, 0)
        if not self.line:
            for k in range(here.nz - 1):
                self.straight(k).wait_send()
            return
        for z in range(here.nz):
            for sems, slot, sign in self.flows():

                @pl.when(sign * (z - here.z) > 0)
                def _():
                    self.along(z, sems, slot, sign).wait_send()


def comm_params(name_id, mib):
    return pltpu.CompilerParams(collective_id=name_id, has_side_effects=True, vmem_limit_bytes=mib * MIB)


def comm_cost(us):
    return pl.CostEstimate(flops=0, bytes_accessed=us * 3_000_000, transcendentals=0)


def entry_kernel(
    dims, small_ref, pick_ref, x_ref, win_ref, wdt_ref, wout_ref, wx_ref, chan_ref,
    modes_out, gain_out, normal_out, win_out, wdt_out, wout_out, wx_out, chan_out,
    slots, own, smalls, cols, keep, lows, weights, *gathers,
):
    here = Place(dims)
    rows_d = win_ref.shape[1]
    rows_e = wdt_ref.shape[1]
    chan = win_out.shape[2] // 2
    greet_all(here)

    def small_copy(k):
        peer = here.of_index(lax.rem(here.i + k, here.devices))
        return remote(small_ref, slots.at[here.i], smalls.at[k, 0], smalls.at[k, 1], peer)

    def send_small(k, carry):
        small_copy(k).start()
        return carry

    lax.fori_loop(1, here.devices, send_small, 0)
    slots[here.i] = small_ref[...]

    def rows_of(g, low):
        return win_out.at[:, pl.ds(pl.multiple_of((g * here.nl + low) * rows_d, rows_d), rows_d), :]

    def cols_of(g):
        dst = rows_of(here.g, here.l)
        out = []
        for side in range(2):
            at = pl.ds(pl.multiple_of(side * INNER + g * chan, chan), chan)
            out.append((win_ref.at[:, :, at], dst.at[:, :, pl.ds(side * chan, chan)]))
        return out

    def send_cols(z, r):
        g = here.in_plane(z, r)
        for side, (src, dst) in enumerate(cols_of(g)):
            to = cols.at[side, z * plane + r, 0]
            there = cols.at[side, here.z * plane + r, 1]
            remote(src, dst, to, there, here.of_group(g, here.l)).start()

    plane = NX * here.ny

    def own_copies():
        out = [
            pltpu.make_async_copy(src, dst, keep.at[5 * side]) for side, (src, dst) in enumerate(cols_of(here.g))
        ]
        for n, (src, dst) in enumerate(shared(here.l)):
            out.append(pltpu.make_async_copy(src, dst, keep.at[n + 1]))
        return out

    def shared(low):
        rows = pl.ds(pl.multiple_of(low * rows_e, rows_e), rows_e)
        return (
            (wdt_ref, wdt_out.at[:, rows, :]),
            (wout_ref, wout_out.at[:, rows, :]),
            (wx_ref, lanes_at(wx_out, low, rows_e)),
            (chan_ref, lanes_at(chan_out, low, rows_e)),
        )

    def low_copies(k):
        peer = here.low_peer(k)
        return [
            remote(src, dst, weights.at[k, n, 0], weights.at[k, n, 1], peer)
            for n, (src, dst) in enumerate(shared(here.l))
        ]

    def own_forward(k):
        return [
            remote(src, dst, lows.at[k, here.g + side * here.groups, 0], lows.at[k, here.g + side * here.groups, 1], here.low_peer(k))
            for side, (src, dst) in enumerate(cols_of(here.g))
        ]

    def col_forward(k, n, src_group, src):
        return remote(src, rows_of(src_group, here.l), lows.at[k, n, 0], lows.at[k, n, 1], here.low_peer(k))

    for copy in own_copies():
        copy.start()
    for k in range(1, here.nl):
        for copy in low_copies(k) + own_forward(k):
            copy.start()

    def wait_small(k, carry):
        small_copy(k).wait_recv()
        return carry

    lax.fori_loop(1, here.devices, wait_small, 0)
    lane = lax.broadcasted_iota(jnp.int32, (1, 128), 1)
    row = jnp.zeros((1, 128), F32)
    for g in range(here.groups):
        row = jnp.where(lane == g, slots[g * here.nl + here.l, MODES : MODES + 1, :], row)
    modes_out[...] = jnp.broadcast_to(row, (8, 128))
    x = x_ref[...].astype(F32)
    scale = lax.rsqrt(jnp.mean(x * x, -1, keepdims=True) + NORM_EPS)
    per = 128 // rows_d
    for t in range(D // 128):
        tile = slots[t * per]
        for n in range(1, per):
            tile = tile + slots[t * per + n]
        row = jnp.sum(tile * pick_ref[...], 0, keepdims=True)
        at = slice(t * 128, (t + 1) * 128)
        gain_out[:, at] = jnp.broadcast_to(row, (8, 128))
        own[:, at] = (x[:, at] * scale * row).astype(BF16)

    gather = Gather(here, own, normal_out, MBLK, gathers, in_line(dims))
    gather.start()

    def send_plane(d):
        def one(r, carry):
            z = jnp.where(lax.rem(r, 2) == 0, here.z_after(d), here.z_before(d))

            @pl.when((z != here.z) | (r > 0))
            def _():
                send_cols(z, r)

            return carry

        lax.fori_loop(0, plane, one, 0)

    send_plane(0)
    for d in range(1, here.nz):
        gather.step(d)
        send_plane(d)
    gather.forward_all()

    def each_source(act):
        def one(n, carry):
            z, r = lax.div(n, plane), lax.rem(n, plane)

            @pl.when((z != here.z) | (r > 0))
            def _():
                act(n, here.in_plane(z, r))

            return carry

        lax.fori_loop(0, here.groups, one, 0)

    def pass_cols(n, g):
        got = rows_of(g, here.l)
        for side in range(2):
            half = got.at[:, :, pl.ds(side * chan, chan)]
            remote(half, half, cols.at[side, n, 0], cols.at[side, n, 1], here.of_group(g, here.l)).wait_recv()
        for k in range(1, here.nl):
            col_forward(k, g, g, got).start()

    each_source(pass_cols)
    gather.end()

    def end_lows(n, g):
        for k in range(1, here.nl):
            mine, theirs = rows_of(g, here.l), rows_of(g, here.low_before(k))
            remote(mine, mine, lows.at[k, g, 0], lows.at[k, g, 1], here.low_peer(k)).wait_send()
            remote(theirs, theirs, lows.at[k, g, 0], lows.at[k, g, 1], here.low_peer(k)).wait_recv()

    def end_sent(n, g):
        for side in range(2):
            half = rows_of(g, here.l).at[:, :, pl.ds(side * chan, chan)]
            remote(half, half, cols.at[side, n, 0], cols.at[side, n, 1], here.x_peer()).wait_send()

    for k in range(1, here.nl):
        for copy in own_forward(k):
            copy.wait()

    def end_small(k, carry):
        small_copy(k).wait_send()
        return carry

    each_source(end_lows)
    each_source(end_sent)
    lax.fori_loop(1, here.devices, end_small, 0)
    for copy in own_copies():
        copy.wait()
    for k in range(1, here.nl):
        for n, (_, got) in enumerate(shared(here.low_before(k))):
            remote(got, got, weights.at[k, n, 0], weights.at[k, n, 1], here.low_peer(k)).wait()


def entry(dims, small, pick, x, win, wdt, wout, wx, chan):
    ns, ny, nl = dims
    groups, devices = ns * ny, ns * ny * nl
    shape = jax.ShapeDtypeStruct

    def tall(ref):
        return shape((MODES, ref.shape[1] * nl, ref.shape[2]), BF16)

    return pl.pallas_call(
        functools.partial(entry_kernel, dims),
        in_specs=[vmem_spec()] * 3 + [any_spec()] * 5,
        out_specs=[vmem_spec()] * 2 + [any_spec()] * 6,
        out_shape=[
            shape((8, 128), F32), shape((8, D), F32), shape((groups, MBLK, D), BF16),
            shape((MODES, D, win.shape[2] // groups), BF16), tall(wdt), tall(wout),
            *[shape(lanes_shape(a.shape[0], nl, a.shape[1]), a.dtype) for a in (wx, chan)],
        ],
        scratch_shapes=[
            VMEM((devices, 8, 128), F32), VMEM((MBLK, D), BF16), DMA((devices, 2)), DMA((2, groups, 2)),
            DMA((6,)), DMA((nl, 2 * groups, 2)), DMA((nl, 4, 2)), *gather_sems(dims),
        ],
        compiler_params=comm_params(1, 60),
        cost_estimate=comm_cost(100),
        name="entry",
    )(small, pick, x, win, wdt, wout, wx, chan)


def column_scratch(dims, rows_d, chan):
    ns, ny, nl = dims
    piece = (ns * ny, MODES, rows_d, chan)
    return [VMEM(piece, F32), VMEM((nl - 1,) + piece, F32), DMA((ns * ny,)), DMA((nl, ns * ny, 2))]


class Columns:
    def __init__(self, here, src, bufs):
        self.here, self.src = here, src
        self.mine, self.theirs, self.keep, self.swap = bufs

    def own_copy(self, n):
        here = self.here
        return pltpu.make_async_copy(self.src.at[:, here.after(n), here.l], self.mine.at[n], self.keep.at[n])

    def swap_copy(self, k, n):
        here = self.here
        part = self.src.at[:, here.after(n), here.low_after(k)]
        sems = self.swap.at[k, n]
        return remote(part, self.theirs.at[k - 1, n], sems.at[0], sems.at[1], here.low_peer(k))

    def begin(self, start, stop):
        def one(n, carry):
            self.own_copy(n).start()
            for k in range(1, self.here.nl):
                self.swap_copy(k, n).start()
            return carry

        lax.fori_loop(start, stop, one, 0)

    def merged(self, n):
        self.own_copy(n).wait()
        total = self.mine[n]
        for k in range(1, self.here.nl):
            self.swap_copy(k, n).wait_recv()
            total = total + self.theirs[k - 1, n]
        return total.astype(BF16)

    def end(self):
        def one(n, carry):
            for k in range(1, self.here.nl):
                self.swap_copy(k, n).wait_send()
            return carry

        lax.fori_loop(0, self.here.groups, one, 0)


def share_kernel(dims, extras, part_ref, *refs):
    here = Place(dims)
    nz, plane = here.nz, NX * here.ny
    more = len(column_scratch(dims, 16, 128)) if extras else 0
    extra_in, refs = refs[:extras], refs[extras:]
    out_ref, extra_out, refs = refs[0], refs[1 : extras + 1], refs[extras + 1 :]
    near, sent, far, res, near_sems, far_sems, back_sems, wide_sems, keep, pairs = refs[:10]
    columns = refs[10 : 10 + more]
    spot = here.x * here.ny + here.y

    def partner(r):
        x = lax.rem(here.x + r // here.ny, NX)
        y = lax.rem(here.y + r % here.ny, here.ny)
        return x * here.ny + y, here.device(here.z, x, y, here.l)

    barrier = pltpu.get_barrier_semaphore()
    peers = [partner(r)[1] for r in range(1, plane)] + [here.z_peer(k) for k in range(1, nz)]
    if extras:
        peers += [here.low_peer(k) for k in range(1, here.nl)]
    for peer in peers:
        pl.semaphore_signal(barrier, inc=1, device_id=peer, device_id_type=pl.DeviceIdType.MESH)
    pl.semaphore_wait(barrier, len(peers))

    def to_near(r):
        at, peer = partner(r)
        return remote(part_ref.at[:, at], near.at[r - 1], near_sems.at[r, 0], near_sems.at[r, 1], peer)

    def to_far(k):
        return remote(sent.at[here.z_after(k)], far.at[k - 1], far_sems.at[k, 0], far_sems.at[k, 1], here.z_peer(k))

    def back_far(k, z):
        return remote(res, out_ref.at[z, spot], back_sems.at[k, 0], back_sems.at[k, 1], here.z_peer(k))

    def back_near(r, at):
        src = out_ref.at[:, spot]
        return remote(src, out_ref.at[:, at], wide_sems.at[r, 0], wide_sems.at[r, 1], partner(r)[1])

    def swaps(k):
        to = here.low_after(k)
        return [
            remote(src.at[:, to], dst.at[k - 1], pairs.at[k, n, 0], pairs.at[k, n, 1], here.low_peer(k))
            for n, (src, dst) in enumerate(zip(extra_in[1:], extra_out[1:]))
        ]

    for r in range(1, plane):
        to_near(r).start()
    for r in range(1, plane):
        to_near(r).wait_recv()

    def total(z):
        out = part_ref[z, spot].astype(F32)
        for r in range(1, plane):
            out = out + near[r - 1, z].astype(F32)
        return out

    for k in range(1, nz):
        z = here.z_after(k)
        sent[z] = total(z).astype(BF16)
        to_far(k).start()
    if extras:
        column = Columns(here, extra_in[0], columns)
        column.begin(0, here.groups)
    mine = total(here.z)
    for k in range(1, nz):
        to_far(k).wait_recv()
        mine = mine + far[k - 1].astype(F32)
    res[...] = mine.astype(BF16)
    own = pltpu.make_async_copy(res, out_ref.at[here.z, spot], keep.at[0])
    own.start()
    for k in range(1, nz):
        back_far(k, here.z).start()
    own.wait()
    for k in range(1, nz):
        back_far(k, here.z_before(k)).wait_recv()
    for r in range(1, plane):
        back_near(r, spot).start()
    if extras:

        def merge(n, carry):
            extra_out[0][here.after(n)] = column.merged(n)
            return carry

        lax.fori_loop(0, here.groups, merge, 0)
    for r in range(1, plane):
        back_near(r, partner(r)[0]).wait()
        to_near(r).wait_send()
    for k in range(1, nz):
        to_far(k).wait_send()
        back_far(k, here.z).wait_send()
    if extras:
        column.end()
        for k in range(1, here.nl):
            for copy in swaps(k):
                copy.wait()


def share(dims, name_id, part, extras=()):
    ns, ny, nl = dims
    nz, plane = ns // NX, NX * ny
    shape = jax.ShapeDtypeStruct
    block = (XCOLS, MBLK)
    far = [shape((nl - 1, e.shape[0]) + e.shape[2:], F32) for e in extras[1:]]
    far_specs = [any_spec()] * len(far)
    if extras:
        far = [shape((ns * ny, MODES) + extras[0].shape[3:], BF16)] + far
        far_specs = [vmem_spec()] + far_specs
    return pl.pallas_call(
        functools.partial(share_kernel, dims, len(extras)),
        in_specs=[vmem_spec()] + [any_spec()] * len(extras),
        out_specs=[any_spec()] + far_specs,
        out_shape=[shape((nz, plane) + block, BF16)] + far,
        scratch_shapes=[
            VMEM((plane - 1, nz) + block, BF16), VMEM((nz,) + block, BF16), VMEM((nz - 1,) + block, BF16),
            VMEM(block, BF16), DMA((plane, 2)), DMA((nz, 2)), DMA((nz, 2)), DMA((plane, 2)), DMA((1,)),
            DMA((nl, max(len(extras), 1), 2)),
        ]
        + (column_scratch(dims, extras[0].shape[3], extras[0].shape[4]) if extras else []),
        compiler_params=comm_params(name_id, 60),
        cost_estimate=comm_cost(30),
        name="share",
    )(part.reshape((nz, plane) + block), *extras)


class Staged:
    def __init__(self, dims, parts):
        self.ns, self.ny, _ = dims
        self.nz = self.ns // NX
        self.parts = parts
        self.z = lax.axis_index("seq") // NX

    def plane(self):
        out = []
        for r in range(1, NX * self.ny):
            dx, dy = r // self.ny, r % self.ny
            moves = []
            for g in range(self.ns * self.ny):
                z, x, y = g // self.ny // NX, g // self.ny % NX, g % self.ny
                moves.append((g, (z * NX + (x + dx) % NX) * self.ny + (y + dy) % self.ny))
            out.append(lax.ppermute(self.parts[r], GROUP, moves))
        return out

    def line(self, got):
        total = self.parts[0].astype(F32)
        for piece in got:
            total = total + piece.astype(F32)
        return total.astype(BF16)

    def along(self, line):
        out = [lax.dynamic_index_in_dim(line, self.z, 0, keepdims=False)]
        for k in range(1, self.nz):
            moves = [(s, ((s // NX + k) % self.nz) * NX + s % NX) for s in range(self.ns)]
            piece = lax.dynamic_index_in_dim(line, (self.z + k) % self.nz, 0, keepdims=False)
            out.append(lax.ppermute(piece, "seq", moves))
        return out


def exit_kernel(
    dims, modes_ref, joint_ref, w_ref, ing_ref, dtg_ref, outg_ref, xg_ref, suma_ref, sumb_ref,
    x_ref, cot_ref, gain_ref, pick_ref,
    grad_out, gsum_out, ready_out, dtg_out, outg_out, xg_out, suma_out, sumb_out,
    part_ref, gparts, gslots, pairs, smalls, *bufs,
):
    here = Place(dims)
    rows_d, chan = ing_ref.shape[3], ing_ref.shape[4]
    rows_e = dtg_ref.shape[2]
    more = len(column_scratch(dims, 16, 128))
    columns, bufs = bufs[:more], bufs[more:]
    greet_all(here)
    nz, plane = here.nz, NX * here.ny
    reduce = Reduce(here, part_ref, MBLK, bufs, False)
    column = Columns(here, ing_ref, columns)

    def pair_copies(k):
        to = here.low_after(k)
        peer = here.low_peer(k)
        out = []
        for n, (src, dst) in enumerate(((dtg_ref, dtg_out), (outg_ref, outg_out))):
            out.append(remote(src.at[:, to], dst.at[k - 1], pairs.at[k, n, 0], pairs.at[k, n, 1], peer))
        for n, (src, dst) in enumerate(((xg_ref, xg_out), (suma_ref, suma_out), (sumb_ref, sumb_out))):
            sems = pairs.at[k, n + 2]
            out.append(remote(lanes_at(src, to, rows_e), dst.at[k - 1], sems.at[0], sems.at[1], peer))
        return out

    def first(k):
        z = reduce.target(k)

        def one(p, carry):
            x, y = lax.div(p, here.ny), lax.rem(p, here.ny)
            block = here.group(z, x, y)
            product = nt_dot(joint_ref[block], w_ref[modes_ref[block]])
            part_ref[z, x, y] = product.astype(BF16)
            return carry

        lax.fori_loop(0, plane, one, 0)
        reduce.first(k)

    for k in range(min(3, nz)):
        first(k)
    for k in range(nz):
        if k + 3 < nz:
            first(k + 3)
        reduce.second(k)
        if k > 0:
            reduce.third(k - 1)
        column.begin(k * plane, (k + 1) * plane)
    for low in range(1, here.nl):
        for copy in pair_copies(low):
            copy.start()

    def merge(n, carry):
        ready_out[here.after(n)] = column.merged(n)
        return carry

    lax.fori_loop(0, here.groups, merge, 0)
    reduce.last()

    acc = reduce.acc
    x = x_ref[...].astype(F32)
    scale = lax.rsqrt(jnp.mean(x * x, -1, keepdims=True) + NORM_EPS)
    back = acc[...]
    weighted = back * gain_ref[0:1, :]
    dots = jnp.mean(weighted * x, -1, keepdims=True)
    back_x = scale * weighted - x * (scale * scale * scale) * dots
    grad_out[...] = (cot_ref[...].astype(F32) + back_x).astype(BF16)
    felt = jnp.sum(back * x * scale, 0, keepdims=True)
    for t in range(D // 128):
        gparts[t] = felt[:, t * 128 : (t + 1) * 128] * pick_ref[...]

    def small_copy(k):
        i = lax.rem(here.i + k, here.devices)
        src = gparts.at[lax.div(i * rows_d, 128)]
        return remote(src, gslots.at[here.i], smalls.at[k, 0], smalls.at[k, 1], here.of_index(i))

    def send_small(k, carry):
        small_copy(k).start()
        return carry

    lax.fori_loop(1, here.devices, send_small, 0)
    gslots[here.i] = gparts[lax.div(here.i * rows_d, 128)]
    reduce.end()
    column.end()
    for k in range(1, here.nl):
        for copy in pair_copies(k):
            copy.wait()
    def end_small(k, carry):
        small_copy(k).wait()
        return carry

    lax.fori_loop(1, here.devices, end_small, 0)
    gsum_out[...] = jnp.sum(gslots[...], 0)


def leave(dims, modes, joint, w_in, ing, swapped, rest, x, cot, gain, pick):
    ns, ny, nl = dims
    groups, devices = ns * ny, ns * ny * nl
    shape = jax.ShapeDtypeStruct
    rows_d, chan, rows_e = ing.shape[3], ing.shape[4], swapped[0].shape[2]
    return pl.pallas_call(
        functools.partial(exit_kernel, dims),
        in_specs=[pl.BlockSpec(memory_space=pltpu.SMEM)] + [vmem_spec()] * 2 + [any_spec()] * 6 + [vmem_spec()] * 4,
        out_specs=[vmem_spec()] * 3 + [any_spec()] * 5,
        out_shape=[
            shape((MBLK, D), BF16), shape((8, 128), F32), shape((groups, MODES, rows_d, chan), BF16),
            *[shape((nl - 1, MODES) + part.shape[2:], F32) for part in swapped],
            *[shape((nl - 1, part.shape[-2], rows_e), F32) for part in rest],
        ],
        scratch_shapes=[
            VMEM((ns // NX, NX, ny, MBLK, D), BF16),
            VMEM((D // 128, 8, 128), F32), VMEM((devices, 8, 128), F32), DMA((nl, 5, 2)), DMA((devices, 2)),
            *column_scratch(dims, rows_d, chan),
            *reduce_scratch(dims, MBLK, D, BF16),
        ],
        compiler_params=comm_params(4, 63),
        cost_estimate=comm_cost(100),
        name="leave",
    )(modes, joint, w_in, ing, *swapped, *rest, x, cot, gain, pick)


def body(
    tokens, modality, cotangent, in_weight, x_weight, dt_weight, out_weight, norm_gain, channel_params,
    in_first, in_second, x_first, x_second, dt_first, dt_second, out_first, out_second,
    gain_first, gain_second, chan_first, chan_second,
):
    nb, seqs, los = lax.axis_size("seq"), lax.axis_size("hi"), lax.axis_size("lo")
    dims = (nb, seqs, los)
    groups = nb * seqs
    chan = INNER // groups
    rows_d = in_weight.shape[0]
    rows_e = x_weight.shape[0]
    plan = Plan(nb, seqs, chan)
    low = lax.axis_index("lo")
    index = (lax.axis_index("seq") * seqs + lax.axis_index("hi")) * los + low
    lane = lax.rem(index * rows_d, 128)

    mode_here = modality[0, 0]
    small = jnp.zeros((8, 128), F32)
    small = lax.dynamic_update_slice(small, rounded(norm_gain.T), (0, lane))
    small = small.at[MODES].set(mode_here.astype(F32))
    pick = (mode_here == lax.broadcasted_iota(jnp.int32, (8, 128), 0)).astype(F32)

    in_cols = in_weight.astype(BF16).swapaxes(0, 1)
    x_low = x_weight.astype(BF16).transpose(1, 2, 0).reshape(MODES * XCOLS, rows_e)
    dt_low = dt_weight.astype(BF16).swapaxes(0, 1)
    out_low = out_weight.astype(BF16).swapaxes(0, 1)
    chan_low = jnp.pad(rounded(channel_params).T, ((0, PAR_ROWS - channel_params.shape[1]), (0, 0)))
    mode_row, gain, normal, w_in, w_dt, w_out, w_x, par = entry(
        dims, small, pick, tokens[0], in_cols, dt_low, out_low, x_low, chan_low
    )
    modes = mode_row[0, :groups].astype(jnp.int32)
    w_x = lanes_join(w_x).reshape(MODES, XCOLS, chan)
    par = lanes_join(par)
    rates = -jnp.exp(par[PAR_RATES : PAR_RATES + STATE])
    rates_f = plan.fold_rates(rates / LN2)
    select = jnp.asarray(plan.select(), BF16)

    cot_here, _ = lax.optimization_barrier((cotangent[0], gain))
    cot = lax.all_gather(cot_here, GROUP, axis=0)

    inner, gate, pre, act, proj_part = front(plan, modes, normal, w_in, w_x, par)
    (proj,) = share(dims, 2, proj_part)
    proj = proj.reshape(groups, XCOLS, MBLK)
    spot = jnp.stack([lax.axis_index("seq") % NX, lax.axis_index("hi")]).astype(jnp.int32)
    scanned, mixed, before, last, *out_parts = forward_scan(
        plan, jnp.concatenate([modes, spot]), proj, act, gate, w_dt, w_out, par, rates_f, select
    )
    cot, out_parts = lax.optimization_barrier((cot, out_parts))
    staged = Staged(dims, out_parts)
    crossed = staged.plane()

    bact, bgate, bproj_part, dt_g, out_g, gate_g, sums_a = backward_scan(
        plan, modes, cot, normal, proj, act, gate, scanned, mixed, before, last, w_dt, w_out, par, rates_f, select
    )
    dt_g = dt_g.reshape(MODES, los, rows_e, RANK)
    out_g = out_g.reshape(MODES, los, rows_e, D)
    gate_g = gate_g.reshape(MODES, groups, los, rows_d, chan)
    crossed, bproj_part = lax.optimization_barrier((crossed, bproj_part))
    bproj, gate_ready = share(dims, 3, bproj_part, (gate_g,))
    bproj = bproj.reshape(groups, XCOLS, MBLK)
    gate_grad = lax.all_to_all(gate_ready, GROUP, 0, 0)
    crossed, bproj = lax.optimization_barrier((crossed, bproj))
    pieces = staged.along(staged.line(crossed))
    joint, in_g, x_g, sums_b = tail(
        plan, modes, bproj, bact, bgate, pre, act, inner, normal, w_x, par
    )
    rest = (x_g.reshape(MODES * XCOLS, chan), sums_a, sums_b)
    input_grad, gain_sum, inner_ready, dt_far, out_far, *rest_far = leave(
        dims, modes, joint, w_in, in_g.reshape(MODES, groups, los, rows_d, chan), (dt_g, out_g),
        tuple(lanes_split(part, los) for part in rest), tokens[0], cotangent[0], gain, pick,
    )

    inner_ready, gate_grad, pieces, gain_sum, dt_far, out_far, rest_far = lax.optimization_barrier(
        (inner_ready, gate_grad, pieces, gain_sum, dt_far, out_far, rest_far)
    )
    inner_grad = lax.all_to_all(inner_ready, GROUP, 0, 0)

    def merged(near, far):
        return lax.dynamic_index_in_dim(near, low, 1, keepdims=False) + jnp.sum(far, 0)

    in_grad = jnp.concatenate(
        [half.transpose(2, 1, 0, 3).reshape(rows_d, MODES, INNER) for half in (inner_grad, gate_grad)], 2
    ).astype(F32)
    dt_grad = merged(dt_g, dt_far).swapaxes(0, 1)
    out_grad = merged(out_g, out_far).swapaxes(0, 1)
    x_sum, sum_a, sum_b = (
        lax.dynamic_slice_in_dim(near, low * rows_e, rows_e, 1) + jnp.sum(far, 0) for near, far in zip(rest, rest_far)
    )
    x_grad = x_sum.reshape(MODES, XCOLS, rows_e).transpose(2, 0, 1)
    chan_grad = jnp.concatenate(
        [
            sum_a[:MODES],
            sum_b[CONV : CONV + 1],
            sum_a[MODES : MODES + 1],
            sum_b[:CONV],
            sum_a[SUM_LOG:],
        ],
        0,
    ).T
    gain_grad = lax.dynamic_slice(gain_sum, (0, lane), (MODES, rows_d)).T

    in_new = adam_update(in_weight, in_first, in_second, in_grad, D ** (-0.5))
    x_new = adam_update(x_weight, x_first, x_second, x_grad, INNER ** (-0.5))
    dt_new = adam_update(dt_weight, dt_first, dt_second, dt_grad, RANK ** (-0.5))
    out_new = adam_update(out_weight, out_first, out_second, out_grad, (4 * INNER) ** (-0.5))
    gain_new = adam_update(norm_gain, gain_first, gain_second, gain_grad, SMALL_RATE)
    chan_new = adam_update(channel_params, chan_first, chan_second, chan_grad, CHAN_RATE)
    out_sum = tokens[0].astype(F32)
    for piece in pieces:
        out_sum = out_sum + piece.astype(F32)
    block_out = out_sum.astype(BF16)[None]
    return (
        block_out,
        input_grad[None],
        *in_new,
        in_new[0].astype(BF16),
        *x_new,
        x_new[0].astype(BF16),
        *dt_new,
        dt_new[0].astype(BF16),
        *out_new,
        out_new[0].astype(BF16),
        *gain_new,
        *chan_new,
    )


def solution(mesh):
    seq, batch = mesh.shape["seq"], mesh.shape["batch"]
    high = max(1, min(batch, GROUPS // seq))
    split = Mesh(mesh.devices.reshape(seq, high, batch // high), EVERY)
    token = P(("hi", "lo"), "seq", None)
    wide = P(EVERY, None, None)
    flat = P(EVERY, None)
    return jax.shard_map(
        body,
        mesh=split,
        in_specs=(token, P(("hi", "lo"), "seq"), token) + (wide,) * 4 + (flat,) * 2 + (wide,) * 8 + (flat,) * 4,
        out_specs=(token,) * 2 + (wide,) * 16 + (flat,) * 6,
        check_vma=False,
    )
```
